128 devices in a mesh: seq: 8 (over z, core), tp: 16 (over y, x).
Axes of the slice: x: 4, y: 4, z: 4, core: 2. Of those that a mesh axis runs over, the one named last changes fastest.
Arguments:
- block_input: float32 [2, 8192, 1024], P(None, 'seq'), may hold values from -6 to 6
- first_gain: float32 [1024], replicated, may hold values from 0.1 to 1.9
- in_weight: bfloat16 [1024, 3, 1024], P(None, None, 'tp'), may hold values from -0.1875 to 0.1875
- conv_taps: float32 [3, 1024], P(None, 'tp'), may hold values from -2.5 to 2.5
- out_weight: bfloat16 [1024, 1024], P('tp'), may hold values from -0.1875 to 0.1875
- second_gain: float32 [1024], replicated, may hold values from 0.1 to 1.9
- gate_weight: bfloat16 [1024, 4608], P(None, 'tp'), may hold values from -0.1875 to 0.1875
- up_weight: bfloat16 [1024, 4608], P(None, 'tp'), may hold values from -0.1875 to 0.1875
- down_weight: bfloat16 [4608, 1024], P('tp'), may hold values from -0.09375 to 0.09375
- doc_starts: int32 [2, 8], replicated, may hold values from 0 to 8191, as said below
- out_cotangent: float32 [2, 8192, 1024], P(None, 'seq'), may hold values from -6 to 6
Outputs:
- block_output: float32 [2, 8192, 1024], P(None, 'seq')
- input_grad: float32 [2, 8192, 1024], P(None, 'seq')
- first_gain_grad: float32 [1024], replicated
- in_weight_grad: float32 [1024, 3, 1024], P(None, None, 'tp')
- conv_taps_grad: float32 [3, 1024], P(None, 'tp')
- out_weight_grad: float32 [1024, 1024], P('tp')
- second_gain_grad: float32 [1024], replicated
- gate_weight_grad: float32 [1024, 4608], P(None, 'tp')
- up_weight_grad: float32 [1024, 4608], P(None, 'tp')
- down_weight_grad: float32 [4608, 1024], P('tp')
The draws below stay inside these ranges and needn't reach their ends.
Inputs may be any that keep to these rules, and one draw needn't show every extreme that they name: `doc_starts`: each row lists the first positions of the 8 documents packed into one sequence, strictly increasing, the first one 0; the last document ends at 8192.
All inputs are finite; a program needn't handle non-finite values.
Results may differ from the reference program's by a relative error of at most 0.024.
Values may be sent and summed in bfloat16 or wider, within the bound.
No kernel may reach another device: no remote copies, remote signals or barrier semaphores. Data moves between devices by JAX's collectives and lax.ppermute only.
A program may use at most 192 MiB of HBM per device.

```python
import jax
import jax.numpy as jnp
from jax import lax

D = 1024
FF = 4608
SEQS = 2
DOCS = 8
SEG = 1024
LEN = 8192


def draw_doc_starts(key, part):
    key = jax.random.fold_in(key, 7)
    row_keys = jax.random.split(key, SEQS)
    span = SEG - 1

    def one_row(row_key):
        picked = jax.random.permutation(row_key, 2 * span)[:DOCS - 1].astype(jnp.int32)
        placed = jnp.where(picked < span, picked + 1, LEN - SEG + 1 + (picked - span))
        return jnp.concatenate([jnp.zeros((1,), jnp.int32), jnp.sort(placed).astype(jnp.int32)])
    return jax.vmap(one_row)(row_keys)


def shard_levels(stream_key, extent, shards, smallest, largest):
    level = 1.0
    for position, blocks in shards:
        steps = jax.random.uniform(jax.random.fold_in(jax.random.fold_in(stream_key, 6), position), (blocks,), jnp.float32, smallest / len(shards), largest / len(shards))
        level = level * jnp.repeat(jnp.exp(steps), extent[position] // blocks).reshape((-1,) + (1,) * (len(extent) - 1 - position))
    return level


def bell_draw(stream_key, dims, scale, limit, pieces=(), kind=jnp.bfloat16):
    level = shard_levels(stream_key, dims, pieces, -0.22, 0.18) if pieces else 1.0
    result = jax.random.normal(stream_key, dims, jnp.float32) * scale * level
    return jnp.minimum(jnp.maximum(result, -limit), limit).astype(kind)


def setup_inputs(seed: int = 0) -> dict:
    keys = jax.random.split(jax.random.key(seed), 12)
    block_input = bell_draw(keys[0], (SEQS, LEN, D), 1.0, 6.0, ((1, 8),), jnp.float32)
    first_gain = jnp.clip(1.0 + 0.18 * jax.random.normal(keys[1], (D,), jnp.float32), 0.1, 1.9)
    in_weight = bell_draw(keys[2], (D, 3, D), D ** -0.5, 0.1875, ((2, 16),))
    conv_taps = bell_draw(keys[3], (3, D), 0.5, 2.5, ((1, 16),), jnp.float32)
    out_weight = bell_draw(keys[4], (D, D), D ** -0.5, 0.1875, ((0, 16),))
    second_gain = jnp.clip(1.0 + 0.18 * jax.random.normal(keys[5], (D,), jnp.float32), 0.1, 1.9)
    gate_weight = bell_draw(keys[6], (D, FF), D ** -0.5, 0.1875, ((1, 16),))
    up_weight = bell_draw(keys[7], (D, FF), D ** -0.5, 0.1875, ((1, 16),))
    down_weight = bell_draw(keys[8], (FF, D), FF ** -0.5, 0.09375, ((0, 16),))
    doc_starts = draw_doc_starts(jax.random.fold_in(keys[11], 71), 0)
    out_cotangent = bell_draw(keys[10], (SEQS, LEN, D), 1.0, 6.0, ((1, 8),), jnp.float32)
    return dict(block_input=block_input, first_gain=first_gain, in_weight=in_weight, conv_taps=conv_taps, out_weight=out_weight, second_gain=second_gain, gate_weight=gate_weight, up_weight=up_weight, down_weight=down_weight, doc_starts=doc_starts, out_cotangent=out_cotangent)


epsilon = 1e-05

@jax.custom_vjp
def low(v):
    return lax.optimization_barrier(v.astype(jnp.bfloat16)).astype(jnp.float32)

@jax.custom_vjp
def low_back(v):
    return v

def low_keep(v):
    return (low(v), None)

def low_pass(kept, grad):
    return (grad,)

def back_keep(v):
    return (v, None)

def back_low(kept, grad):
    return (low(grad),)
low.defvjp(low_keep, low_pass)
low_back.defvjp(back_keep, back_low)

def doc_index(doc_starts, positions):
    hits = (doc_starts[:, None, :] <= positions[None, :, None]).astype(jnp.int32)
    return lax.optimization_barrier(jnp.sum(hits, axis=-1)) - 1

def reference(block_input, first_gain, in_weight, conv_taps, out_weight, second_gain, gate_weight, up_weight, down_weight, doc_starts, out_cotangent):
    highest = lax.Precision.HIGHEST
    positions = jnp.arange(LEN, dtype=jnp.int32)
    current = doc_index(doc_starts, positions)
    one_back = (doc_index(doc_starts, positions - 1) == current).astype(jnp.float32)[..., None]
    two_back = (doc_index(doc_starts, positions - 2) == current).astype(jnp.float32)[..., None]

    def forward(inputs, gain_one, weight_in, taps, weight_out, gain_two, weight_gate, weight_up, weight_down):
        inverse_one = lax.rsqrt(lax.optimization_barrier(jnp.mean(inputs * inputs, axis=-1, keepdims=True)) + epsilon)
        normed1 = low(inputs * inverse_one * gain_one)
        projected = low_back(jnp.einsum('std,dgc->stgc', normed1, weight_in, precision=highest))
        b_gate = projected[:, :, 0]
        c_gate = projected[:, :, 1]
        x_gate = projected[:, :, 2]
        product = low(b_gate * x_gate)
        prev_one = jnp.pad(product, ((0, 0), (1, 0), (0, 0)))[:, :-1]
        prev_two = jnp.pad(product, ((0, 0), (2, 0), (0, 0)))[:, :-2]
        convolved = taps[0] * product + taps[1] * one_back * prev_one + taps[2] * two_back * prev_two
        mixer_in = low(c_gate * convolved)
        mixer_out = low_back(jnp.einsum('stc,cd->std', mixer_in, weight_out, precision=highest))
        residual = inputs + mixer_out
        inverse_two = lax.rsqrt(lax.optimization_barrier(jnp.mean(residual * residual, axis=-1, keepdims=True)) + epsilon)
        normed2 = low(residual * inverse_two * gain_two)
        gate_proj = low_back(jnp.einsum('std,dh->sth', normed2, weight_gate, precision=highest))
        up_proj = low_back(jnp.einsum('std,dh->sth', normed2, weight_up, precision=highest))
        hidden = low(jax.nn.silu(gate_proj) * up_proj)
        ffn_out = low_back(jnp.einsum('sth,hd->std', hidden, weight_down, precision=highest))
        return residual + ffn_out
    block_output, pullback = jax.vjp(forward, block_input, first_gain, in_weight.astype(jnp.float32), conv_taps, out_weight.astype(jnp.float32), second_gain, gate_weight.astype(jnp.float32), up_weight.astype(jnp.float32), down_weight.astype(jnp.float32))
    grads = pullback(out_cotangent)
    return (block_output, grads[0], grads[1], grads[2], grads[3], grads[4], grads[5], grads[6], grads[7], grads[8])
```

```python
import jax
import jax.numpy as jnp
from jax import lax
from jax.experimental import pallas as pl
from jax.experimental.pallas import tpu as pltpu
from jax.sharding import Mesh
from jax.sharding import PartitionSpec as P

epsilon = 1e-05
SEQ = ("z", "core")
TP = ("y", "x")
ALL = SEQ + TP
RING = 4
TPS = RING * RING
f32 = jnp.float32
bf16 = jnp.bfloat16


def turn(value, axis, steps):
    return lax.ppermute(value, axis, [(i, (i + steps) % RING) for i in range(RING)])


def ring_gather(value, axis):
    return [value, turn(value, axis, 3), turn(value, axis, 2), turn(value, axis, 1)]


def ring_gather_relay(value, axis):
    half = value.shape[0] // 2
    behind, ahead = turn(value, axis, 1), turn(value, axis, 3)
    top, bottom = turn(behind[:half], axis, 1), turn(ahead[half:], axis, 3)
    return [value, ahead, jnp.concatenate([top, bottom], axis=0), behind]


def ring_scatter(blocks, axis):
    received = [turn(blocks[k], axis, k) for k in (1, 2, 3)]
    total = blocks[0].astype(f32)
    for block in received:
        total = total + block.astype(f32)
    return total


def ring_scatter_relay(blocks, axis):
    half = blocks[2].shape[0] // 2
    low = turn(blocks[2][:half], axis, 1).astype(f32)
    high = turn(blocks[2][half:], axis, 3).astype(f32)
    first, third = blocks[1], blocks[3]
    first = jnp.concatenate([(first[:half].astype(f32) + low).astype(bf16), first[half:]], axis=0)
    third = jnp.concatenate([third[:half], (third[half:].astype(f32) + high).astype(bf16)], axis=0)
    return blocks[0].astype(f32) + turn(first, axis, 1).astype(f32) + turn(third, axis, 3).astype(f32)


def ring_total(value, axis):
    a, b, c, d = (part.astype(f32) for part in ring_gather(value, axis))
    return (a + c) + (b + d)


def plane_gather(value):
    half = value.shape[0] // 2
    top, bottom = value[:half], value[half:]
    top_x = jnp.concatenate(ring_gather(top, "x"), axis=0)
    bottom_y = jnp.concatenate(ring_gather(bottom, "y"), axis=0)
    return ring_gather_relay(top_x, "y"), ring_gather_relay(bottom_y, "x")


def plane_scatter(chunks_a, chunks_b):
    top_x = ring_scatter_relay(chunks_a, "y").astype(bf16)
    bottom_y = ring_scatter_relay(chunks_b, "x").astype(bf16)
    rows = top_x.shape[0] // RING
    top = ring_scatter([top_x[rows * k : rows * (k + 1)] for k in range(RING)], "x")
    bottom = ring_scatter([bottom_y[rows * k : rows * (k + 1)] for k in range(RING)], "y")
    return jnp.concatenate([top, bottom], axis=0)


def plane_exchange(blocks):
    moved = [blocks[:, 0]] + [None] * 3
    for k in (1, 2, 3):
        moved[RING - k] = turn(blocks[:, k], "x", k)
    moved = jnp.stack(moved, axis=1)
    out = [moved[0]] + [None] * 3
    for k in (1, 2, 3):
        out[RING - k] = turn(moved[k], "y", k)
    return jnp.stack(out, axis=0)


def rolled(value, axis, start):
    twice = jnp.concatenate([value, value], axis=axis)
    return lax.dynamic_slice_in_dim(twice, start, RING, axis=axis)


def to_relative(value):
    y, x = lax.axis_index("y"), lax.axis_index("x")
    return rolled(rolled(value, 0, y), 1, x)


def to_absolute(value):
    y, x = lax.axis_index("y"), lax.axis_index("x")
    return rolled(rolled(value, 0, (RING - y) % RING), 1, (RING - x) % RING)


def plane_tables():
    y, x = lax.axis_index("y"), lax.axis_index("x")
    i = jnp.arange(TPS, dtype=jnp.int32)
    first, second = i // RING, i % RING
    from_a = ((first + y) % RING) * RING + (second + x) % RING
    from_b = ((second + y) % RING) * RING + (first + x) % RING
    a, b = (first - y) % RING, (second - x) % RING
    return from_a, from_b, a * RING + b, b * RING + a


def relative_rows(rows, from_a, from_b):
    half, width = rows.shape[0] // TPS // 2, rows.shape[1]
    view = rows.reshape(2 * TPS, half, width)

    def body(ia, ib, top, bottom, out_a, out_b):
        out_a[...] = top[...].astype(bf16)
        out_b[...] = bottom[...].astype(bf16)

    block = (1, half, width)
    return pl.pallas_call(
        body,
        grid_spec=pltpu.PrefetchScalarGridSpec(
            num_scalar_prefetch=2,
            grid=(TPS,),
            in_specs=[
                pl.BlockSpec(block, lambda i, ia, ib: (2 * ia[i], 0, 0)),
                pl.BlockSpec(block, lambda i, ia, ib: (2 * ib[i] + 1, 0, 0)),
            ],
            out_specs=[pl.BlockSpec(block, lambda i, ia, ib: (i, 0, 0))] * 2,
        ),
        out_shape=[jax.ShapeDtypeStruct((TPS, half, width), bf16)] * 2,
        name="relative_rows",
    )(from_a, from_b, view, view)


def absolute_rows(part_a, part_b, to_a, to_b):
    _, half, width = part_a.shape

    def body(ia, ib, top, bottom, out):
        out[0, :half] = top[0].astype(f32)
        out[0, half:] = bottom[0].astype(f32)

    block = (1, half, width)
    out = pl.pallas_call(
        body,
        grid_spec=pltpu.PrefetchScalarGridSpec(
            num_scalar_prefetch=2,
            grid=(TPS,),
            in_specs=[
                pl.BlockSpec(block, lambda i, ia, ib: (ia[i], 0, 0)),
                pl.BlockSpec(block, lambda i, ia, ib: (ib[i], 0, 0)),
            ],
            out_specs=pl.BlockSpec((1, 2 * half, width), lambda i, ia, ib: (i, 0, 0)),
        ),
        out_shape=jax.ShapeDtypeStruct((TPS, 2 * half, width), f32),
        name="absolute_rows",
    )(to_a, to_b, part_a, part_b)
    return out.reshape(TPS * 2 * half, width)


def dot(left, right, left_dim, right_dim, kind=f32):
    out = lax.dot_general(
        left, right, (((left_dim,), (right_dim,)), ((), ())), preferred_element_type=f32
    )
    return out.astype(kind)


def doc_index(doc_starts, positions):
    hits = (doc_starts[:, None, :] <= positions[None, :, None]).astype(jnp.int32)
    return jnp.sum(hits, axis=-1) - 1


def shards(
    block_input,
    first_gain,
    in_weight,
    conv_taps,
    out_weight,
    second_gain,
    gate_weight,
    up_weight,
    down_weight,
    doc_starts,
    out_cotangent,
):
    seqs, seg, width = block_input.shape
    chans = in_weight.shape[2]
    ff = gate_weight.shape[1]
    count = seqs * seg
    own = count // TPS
    per_seq = TPS // seqs
    y, x = lax.axis_index("y"), lax.axis_index("x")
    place = y * RING + x
    seq = lax.axis_index(SEQ)
    from_a, from_b, to_a, to_b = plane_tables()

    positions = seq * seg + jnp.arange(seg, dtype=jnp.int32)
    current = doc_index(doc_starts, positions)
    one_back = (doc_index(doc_starts, positions - 1) == current).astype(f32)
    two_back = (doc_index(doc_starts, positions - 2) == current).astype(f32)

    out_a, out_b = plane_gather(out_weight)
    out_rel_a = jnp.concatenate(out_a, axis=0)
    out_rel_b = jnp.concatenate(out_b, axis=0)
    in_wt = jnp.transpose(in_weight, (1, 2, 0))
    share = chans // 8
    in_share = lax.dynamic_slice_in_dim(in_wt, seq * share, share, axis=1)
    in_all = lax.all_gather(in_share, ALL, axis=0, tiled=False)
    in_all = in_all.reshape(8, TPS, 3, share, width).transpose(2, 1, 0, 3, 4)
    in_all = in_all.reshape(3 * TPS * chans, width)
    taps = jnp.stack(ring_gather(conv_taps, "x"), axis=0)
    taps = jnp.stack(ring_gather(taps, "y"), axis=0)
    taps = to_absolute(taps).reshape(TPS, 3, chans).transpose(1, 0, 2).reshape(3, TPS * chans)

    flat_input = block_input.reshape(count, width)
    inverse_one = lax.rsqrt(jnp.mean(flat_input * flat_input, axis=-1, keepdims=True) + epsilon)
    normed1 = (flat_input * inverse_one * first_gain).astype(bf16)
    last = normed1.reshape(seqs, seg, width)[:, seg - 8 :]
    carried = lax.ppermute(
        last, ALL, [(i, i + TPS) for i in range(7 * TPS)]
    )
    in_flat = in_wt.reshape(3 * chans, width)
    mixer_blocks = []
    for s in range(seqs):
        proj = dot(in_flat, normed1[s * seg : (s + 1) * seg], 1, 1)
        edge = dot(in_flat, carried[s], 1, 1)
        product = (proj[:chans] * proj[2 * chans :]).astype(bf16)
        before = (edge[:chans] * edge[2 * chans :]).astype(bf16)
        extended = jnp.concatenate([before[:, 6:], product], axis=1).astype(f32)
        convolved = (
            conv_taps[0][:, None] * product.astype(f32)
            + conv_taps[1][:, None] * one_back[s] * extended[:, 1 : seg + 1]
            + conv_taps[2][:, None] * two_back[s] * extended[:, :seg]
        )
        mixed = (proj[chans : 2 * chans] * convolved).astype(bf16)
        mixer_blocks.append(mixed.reshape(chans, per_seq, own).transpose(1, 0, 2))
    mixer_blocks = jnp.concatenate(mixer_blocks, axis=0).reshape(RING, RING, chans, own)
    mixer = plane_exchange(to_relative(mixer_blocks))
    half = chans // 2
    mixer_a = mixer[:, :, :half].reshape(TPS * half, own)
    mixer_b = mixer[:, :, half:].transpose(1, 0, 2, 3).reshape(TPS * half, own)

    rows_in = lax.dynamic_slice_in_dim(flat_input, place * own, own, axis=0)
    residual = rows_in + (dot(mixer_a, out_rel_a, 0, 0) + dot(mixer_b, out_rel_b, 0, 0))
    inverse_two = lax.rsqrt(jnp.mean(residual * residual, axis=-1, keepdims=True) + epsilon)
    normed2 = (residual * inverse_two * second_gain).astype(bf16)

    norm_a, norm_b = plane_gather(normed2)
    grad_a, grad_b = relative_rows(out_cotangent.reshape(count, width), from_a, from_b)
    grad_low = [g.reshape(RING, count // 8, width) for g in (grad_a, grad_b)]
    gate_t, up_t = gate_weight.T, up_weight.T
    both_t = jnp.concatenate([gate_t, up_t], axis=0)
    chunks, halves, hiddens, downs, ups = norm_a + norm_b, [], [], [], []
    for index, chunk in enumerate(chunks):
        low = grad_low[index // RING][index % RING]
        d_hidden = dot(low, down_weight, 1, 1)
        both = dot(chunk, both_t, 1, 1)
        gate, up = both[:, :ff], both[:, ff:]
        sig = jax.nn.sigmoid(gate)
        act = gate * sig
        hidden = (act * up).astype(bf16)
        d_gate = (d_hidden * up * sig * (1.0 + gate * (1.0 - sig))).astype(bf16)
        d_up = (d_hidden * act).astype(bf16)
        d_both = jnp.concatenate([d_gate, d_up], axis=1)
        hiddens.append(hidden)
        halves.append(d_both)
        ups.append(dot(d_both, both_t, 1, 0, bf16))
        downs.append(dot(hidden, down_weight, 1, 0, bf16))
    d_normed2 = plane_scatter(ups[:RING], ups[RING:])
    ffn = plane_scatter(downs[:RING], downs[RING:])
    all_low = jnp.concatenate([g.reshape(count // 2, width) for g in grad_low], axis=0)
    ffn_grads = jnp.concatenate(
        [
            dot(jnp.concatenate(halves, axis=0), jnp.concatenate(chunks, axis=0), 0, 0, bf16),
            dot(jnp.concatenate(hiddens, axis=0), all_low, 0, 0, bf16),
            jnp.zeros((32, width), bf16),
        ],
        axis=0,
    )
    ffn_grads = lax.psum_scatter(ffn_grads, SEQ, scatter_dimension=0, tiled=True)
    ffn_grads = lax.all_gather(ffn_grads, SEQ, axis=0, tiled=True)
    gate_grad = ffn_grads[:ff].astype(f32).T
    up_grad = ffn_grads[ff : 2 * ff].astype(f32).T
    down_grad = ffn_grads[2 * ff : 3 * ff].astype(f32)

    block_a, block_b = plane_gather((residual + ffn).astype(bf16))
    shape = (TPS, own // 2, width)
    block_output = absolute_rows(
        jnp.concatenate(block_a, axis=0).reshape(shape),
        jnp.concatenate(block_b, axis=0).reshape(shape),
        to_a,
        to_b,
    )

    grad_rows = lax.dynamic_slice_in_dim(
        out_cotangent.reshape(count, width), place * own, own, axis=0
    )
    scaled = second_gain * d_normed2
    second_part = jnp.sum(d_normed2 * residual * inverse_two, axis=0)
    d_residual = grad_rows + inverse_two * (
        scaled
        - residual
        * inverse_two
        * inverse_two
        * jnp.mean(scaled * residual, axis=-1, keepdims=True)
    )
    d_low = d_residual.astype(bf16)

    out_abs = jnp.concatenate(
        [
            to_absolute(out_rel_a.reshape(RING, RING, half, width)),
            to_absolute(
                out_rel_b.reshape(RING, RING, half, width).transpose(1, 0, 2, 3)
            ),
        ],
        axis=2,
    ).reshape(TPS * chans, width)
    d_mixer = dot(d_low, out_abs, 1, 1)

    rows_n1 = lax.dynamic_slice_in_dim(normed1, place * own, own, axis=0)
    local_edge = lax.dynamic_slice_in_dim(normed1, place * own - 8, 8, axis=0)
    at_start = place % per_seq == 0
    edge_n1 = jnp.where(at_start, carried[place // per_seq], local_edge)
    again = dot(jnp.concatenate([edge_n1, rows_n1], axis=0), in_all, 1, 1)
    channels = TPS * chans
    b_all, c_all, x_all = (again[:, g * channels : (g + 1) * channels] for g in range(3))
    b_gate, c_gate, x_gate = b_all[8:], c_all[8:], x_all[8:]
    product = (b_all * x_all).astype(bf16).astype(f32)
    rows_one = lax.dynamic_slice_in_dim(one_back.reshape(count, 1), place * own, own, axis=0)
    rows_two = lax.dynamic_slice_in_dim(two_back.reshape(count, 1), place * own, own, axis=0)
    lagged_one = rows_one * product[7 : 7 + own]
    lagged_two = rows_two * product[6 : 6 + own]
    product = product[8:]
    convolved = taps[0] * product + taps[1] * lagged_one + taps[2] * lagged_two

    d_conv = d_mixer * c_gate
    d_cgate = d_mixer * convolved
    lag_one = rows_one * d_conv
    lag_two = rows_two * d_conv
    pairs = []
    for sq in range(8):
        for j in range(TPS):
            if j % per_seq:
                pairs.append((sq * TPS + j, sq * TPS + j - 1))
            elif sq:
                pairs.append((sq * TPS + j, (sq - 1) * TPS + j + per_seq - 1))
    edges = lax.ppermute(jnp.concatenate([lag_one[:2], lag_two[:2]], axis=0), ALL, pairs)
    ahead_one = jnp.concatenate([lag_one[1:], edges[:1]], axis=0)
    ahead_two = jnp.concatenate([lag_two[2:], edges[2:]], axis=0)
    d_product = taps[0] * d_conv + taps[1] * ahead_one + taps[2] * ahead_two
    d_projected = jnp.concatenate(
        [d_product * x_gate, d_cgate, d_product * b_gate], axis=1
    ).astype(bf16)
    d_normed1 = dot(d_projected, in_all, 1, 0)
    rows_inverse = lax.rsqrt(jnp.mean(rows_in * rows_in, axis=-1, keepdims=True) + epsilon)
    scaled_one = first_gain * d_normed1
    first_part = jnp.sum(d_normed1 * rows_in * rows_inverse, axis=0)
    input_rows = d_residual + rows_inverse * (
        scaled_one
        - rows_in
        * rows_inverse
        * rows_inverse
        * jnp.mean(scaled_one * rows_in, axis=-1, keepdims=True)
    )
    input_a, input_b = plane_gather(input_rows.astype(bf16))
    input_grad = absolute_rows(
        jnp.concatenate(input_a, axis=0).reshape(shape),
        jnp.concatenate(input_b, axis=0).reshape(shape),
        to_a,
        to_b,
    )

    small = jnp.stack(
        [
            first_part,
            second_part,
            jnp.sum(d_conv * product, axis=0),
            jnp.sum(d_conv * lagged_one, axis=0),
            jnp.sum(d_conv * lagged_two, axis=0),
        ],
        axis=0,
    )
    small = small + lax.ppermute(small, "core", [(0, 1), (1, 0)])
    small = ring_total(ring_total(ring_total(small, "z"), "y"), "x")
    first_grad, second_grad = small[0], small[1]
    taps_grad = lax.dynamic_slice_in_dim(small[2:], place * chans, chans, axis=1)

    out_part_a = dot(mixer_a, d_low, 1, 0, bf16)
    out_part_b = dot(mixer_b, d_low, 1, 0, bf16)
    step = RING * half
    out_part = plane_scatter(
        [out_part_a[step * k : step * (k + 1)] for k in range(RING)],
        [out_part_b[step * k : step * (k + 1)] for k in range(RING)],
    ).astype(bf16)
    blocks = d_projected.reshape(own, 3, RING, RING, chans).transpose(2, 3, 1, 4, 0)
    blocks = blocks.reshape(RING, RING, 3 * chans, own)
    received = to_absolute(plane_exchange(to_relative(blocks)))
    received = received.reshape(TPS, 3 * chans, own).transpose(1, 0, 2).reshape(3 * chans, count)
    in_part = dot(received, normed1, 1, 0, bf16)
    part = jnp.concatenate([in_part, out_part], axis=0)
    middle = part.shape[0] // 2
    low_half, high_half = part[:middle], part[middle:]
    is_low = lax.axis_index("core") == 0
    theirs = lax.ppermute(jnp.where(is_low, high_half, low_half), "core", [(0, 1), (1, 0)])
    mine = jnp.where(is_low, low_half, high_half).astype(f32) + theirs.astype(f32)
    mine = ring_total(mine.astype(bf16), "z").astype(bf16)
    theirs = lax.ppermute(mine, "core", [(0, 1), (1, 0)])
    total = jnp.concatenate(
        [jnp.where(is_low, mine, theirs), jnp.where(is_low, theirs, mine)], axis=0
    ).astype(f32)
    in_grad = total[: 3 * chans].reshape(3, chans, width).transpose(2, 0, 1)
    out_grad = total[3 * chans :]

    return (
        block_output.reshape(seqs, seg, width),
        input_grad.reshape(seqs, seg, width),
        first_grad,
        in_grad,
        taps_grad,
        out_grad,
        second_grad,
        gate_grad,
        up_grad,
        down_grad,
    )


def solution(mesh):
    grid = Mesh(mesh.devices.reshape(4, 2, RING, RING), ALL)
    return jax.shard_map(
        shards,
        mesh=grid,
        in_specs=(
            P(None, SEQ, None),
            P(),
            P(None, None, TP),
            P(None, TP),
            P(TP, None),
            P(),
            P(None, TP),
            P(None, TP),
            P(TP, None),
            P(),
            P(None, SEQ, None),
        ),
        out_specs=(
            P(None, SEQ, None),
            P(None, SEQ, None),
            P(),
            P(None, None, TP),
            P(None, TP),
            P(TP, None),
            P(),
            P(None, TP),
            P(None, TP),
            P(TP, None),
        ),
        check_vma=False,
    )
```

```python
import jax
import jax.numpy as jnp
from jax import lax
from jax.experimental import pallas as pl
from jax.experimental.pallas import tpu as pltpu
from jax.sharding import Mesh
from jax.sharding import PartitionSpec as P

epsilon = 1e-05
SEQ = ("z", "core")
TP = ("y", "x")
ALL = SEQ + TP
RING = 4
TPS = RING * RING
f32 = jnp.float32
bf16 = jnp.bfloat16


def turn(value, axis, steps):
    return lax.ppermute(value, axis, [(i, (i + steps) % RING) for i in range(RING)])


def ring_gather(value, axis):
    return [value, turn(value, axis, 3), turn(value, axis, 2), turn(value, axis, 1)]


def ring_near(value, axis):
    return turn(value, axis, 3), turn(value, axis, 1)


def ring_far(ahead, behind, axis):
    half = ahead.shape[0] // 2
    return turn(behind[:half], axis, 1), turn(ahead[half:], axis, 3)


def ring_send_far(block, axis):
    half = block.shape[0] // 2
    return turn(block[:half], axis, 1), turn(block[half:], axis, 3)


def ring_send_near(ahead, behind, low, high, axis):
    half = ahead.shape[0] // 2
    ahead_top = (ahead[:half].astype(f32) + low.astype(f32)).astype(bf16)
    behind_bottom = (behind[half:].astype(f32) + high.astype(f32)).astype(bf16)
    ahead = jnp.concatenate([ahead_top, ahead[half:]], axis=0)
    behind = jnp.concatenate([behind[:half], behind_bottom], axis=0)
    return turn(ahead, axis, 1), turn(behind, axis, 3)


def ring_scatter(blocks, axis):
    received = [turn(blocks[k], axis, k) for k in (1, 2, 3)]
    total = blocks[0].astype(f32)
    for block in received:
        total = total + block.astype(f32)
    return total


tied = lax.optimization_barrier


def plane_gather(value, beside=()):
    half = value.shape[0] // 2
    top, bottom = value[:half], value[half:]
    near = tied(ring_near(top, "x") + ring_near(bottom, "y"))
    far = tied(ring_far(near[0], near[1], "x") + ring_far(near[2], near[3], "y"))
    top = jnp.concatenate([top, near[0], far[0], far[1], near[1]], axis=0)
    bottom = jnp.concatenate([bottom, near[2], far[2], far[3], near[3]], axis=0)
    near = ring_near(top, "y") + ring_near(bottom, "x")
    near, beside = tied((near, beside))
    far = tied(ring_far(near[0], near[1], "y") + ring_far(near[2], near[3], "x"))
    return [top, near[0], near[1], bottom, near[2], near[3]], list(far), beside


def plane_scatter(first, last, beside=()):
    middle = last.shape[0] // 2
    moved = tied(ring_send_far(last[:middle], "y") + ring_send_far(last[middle:], "x"))
    top, top_ahead, top_behind, bottom, bottom_ahead, bottom_behind = (
        first[middle * k : middle * (k + 1)] for k in range(6)
    )
    moved = ring_send_near(top_ahead, top_behind, *moved[:2], "y") + ring_send_near(
        bottom_ahead, bottom_behind, *moved[2:], "x"
    )
    moved, beside = tied((moved, beside))
    top = top.astype(f32) + (moved[0].astype(f32) + moved[1].astype(f32))
    bottom = bottom.astype(f32) + (moved[2].astype(f32) + moved[3].astype(f32))
    rows = middle // RING

    def blocks(total):
        low = total.astype(bf16)
        return total[:rows], low[rows : 2 * rows], low[2 * rows : 3 * rows], low[3 * rows :]

    top, top_ahead, top_far, top_behind = blocks(top)
    bottom, bottom_ahead, bottom_far, bottom_behind = blocks(bottom)
    moved = tied(ring_send_far(top_far, "x") + ring_send_far(bottom_far, "y"))
    moved = tied(
        ring_send_near(top_ahead, top_behind, *moved[:2], "x")
        + ring_send_near(bottom_ahead, bottom_behind, *moved[2:], "y")
    )
    top = top + (moved[0].astype(f32) + moved[1].astype(f32))
    bottom = bottom + (moved[2].astype(f32) + moved[3].astype(f32))
    return jnp.concatenate([top, bottom], axis=0), beside


def rolled(value, axis, start):
    twice = jnp.concatenate([value, value], axis=axis)
    return lax.dynamic_slice_in_dim(twice, start, RING, axis=axis)


def swap_cores(value):
    return lax.ppermute(value, "core", [(0, 1), (1, 0)])


CHUNKS = ((0, 0), (0, 1), (0, 3), (1, 0), (1, 1), (1, 3), (0, 2), (1, 2))


def plane_starts(half):
    y, x = lax.axis_index("y"), lax.axis_index("x")
    side = jnp.array([s for s, _ in CHUNKS for _ in range(RING)], jnp.int32)
    outer = jnp.array([k for _, k in CHUNKS for _ in range(RING)], jnp.int32)
    inner = jnp.array([k for _ in CHUNKS for k in range(RING)], jnp.int32)
    row = (jnp.where(side == 0, outer, inner) + y) % RING
    column = (jnp.where(side == 0, inner, outer) + x) % RING
    return (2 * (row * RING + column) + side) * half


def relative_rows(rows, starts):
    half, width = rows.shape[0] // TPS // 2, rows.shape[1]

    def body(table, source, out, held, sems):
        def copy(i):
            start = pl.multiple_of(table[i], half)
            return pltpu.make_async_copy(
                source.at[pl.ds(start, half)], held.at[i], sems.at[i]
            )

        for i in range(2 * TPS):
            copy(i).start()
        for i in range(2 * TPS):
            copy(i).wait()
            out[i * half : (i + 1) * half, :] = held[i].astype(bf16)

    return pl.pallas_call(
        body,
        grid_spec=pltpu.PrefetchScalarGridSpec(
            num_scalar_prefetch=1,
            grid=(1,),
            in_specs=[pl.BlockSpec(memory_space=pl.ANY)],
            out_specs=pl.BlockSpec(memory_space=pltpu.VMEM),
            scratch_shapes=[
                pltpu.VMEM((2 * TPS, half, width), f32),
                pltpu.SemaphoreType.DMA((2 * TPS,)),
            ],
        ),
        out_shape=jax.ShapeDtypeStruct(rows.shape, bf16),
        compiler_params=pltpu.CompilerParams(vmem_limit_bytes=24 * 1024 * 1024),
        cost_estimate=pl.CostEstimate(
            flops=rows.size, bytes_accessed=rows.size * 6, transcendentals=0
        ),
        name="relative_rows",
    )(starts, rows)


def absolute_rows(chunks, starts):
    total, width = sum(chunk.shape[0] for chunk in chunks), chunks[0].shape[1]
    half = total // TPS // 2
    pieces = [(k, j) for k, chunk in enumerate(chunks) for j in range(chunk.shape[0] // half)]

    def body(table, *refs):
        parts, out, held, sems = refs[: len(chunks)], refs[-3], refs[-2], refs[-1]

        def copy(i):
            start = pl.multiple_of(table[i], half)
            return pltpu.make_async_copy(held.at[i], out.at[pl.ds(start, half)], sems.at[i])

        for i, (k, j) in enumerate(pieces):
            held[i] = parts[k][j * half : (j + 1) * half, :].astype(f32)
            copy(i).start()
        for i in range(2 * TPS):
            copy(i).wait()

    return pl.pallas_call(
        body,
        grid_spec=pltpu.PrefetchScalarGridSpec(
            num_scalar_prefetch=1,
            grid=(1,),
            in_specs=[pl.BlockSpec(memory_space=pltpu.VMEM)] * len(chunks),
            out_specs=pl.BlockSpec(memory_space=pl.ANY),
            scratch_shapes=[
                pltpu.VMEM((2 * TPS, half, width), f32),
                pltpu.SemaphoreType.DMA((2 * TPS,)),
            ],
        ),
        out_shape=jax.ShapeDtypeStruct((total, width), f32),
        compiler_params=pltpu.CompilerParams(vmem_limit_bytes=24 * 1024 * 1024),
        cost_estimate=pl.CostEstimate(
            flops=total * width, bytes_accessed=total * width * 6, transcendentals=0
        ),
        name="absolute_rows",
    )(starts, *chunks)


def placed_blocks(chunks):
    rows, width = chunks[0].shape
    block = rows // RING
    y, x = lax.axis_index("y"), lax.axis_index("x")
    i = jnp.arange(TPS, dtype=jnp.int32)
    starts = (((i // RING + y) % RING) * RING + (i + x) % RING) * block

    def body(table, *refs):
        out, sems = refs[RING], refs[RING + 1]

        def copy(i):
            start = pl.multiple_of(table[i], block)
            k = i % RING
            return pltpu.make_async_copy(
                refs[i // RING].at[pl.ds(k * block, block)],
                out.at[pl.ds(start, block)],
                sems.at[i],
            )

        for i in range(TPS):
            copy(i).start()
        for i in range(TPS):
            copy(i).wait()

    return pl.pallas_call(
        body,
        grid_spec=pltpu.PrefetchScalarGridSpec(
            num_scalar_prefetch=1,
            grid=(1,),
            in_specs=[pl.BlockSpec(memory_space=pl.ANY)] * RING,
            out_specs=pl.BlockSpec(memory_space=pl.ANY),
            scratch_shapes=[pltpu.SemaphoreType.DMA((TPS,))],
        ),
        out_shape=jax.ShapeDtypeStruct((TPS * block, width), chunks[0].dtype),
        compiler_params=pltpu.CompilerParams(vmem_limit_bytes=4 * 1024 * 1024),
        cost_estimate=pl.CostEstimate(
            flops=0, bytes_accessed=TPS * block * width * 4, transcendentals=0
        ),
        name="placed_blocks",
    )(starts, *chunks)


def dot(left, right, left_dim, right_dim, kind=f32):
    out = lax.dot_general(
        left, right, (((left_dim,), (right_dim,)), ((), ())), preferred_element_type=f32
    )
    return out.astype(kind)


def doc_index(doc_starts, positions):
    hits = (doc_starts[:, None, :] <= positions[None, :, None]).astype(jnp.int32)
    return jnp.sum(hits, axis=-1) - 1


def shards(
    block_input,
    first_gain,
    in_weight,
    conv_taps,
    out_weight,
    second_gain,
    gate_weight,
    up_weight,
    down_weight,
    doc_starts,
    out_cotangent,
):
    seqs, seg, width = block_input.shape
    chans = in_weight.shape[2]
    ff = gate_weight.shape[1]
    count = seqs * seg
    own = count // TPS
    per_seq = TPS // seqs
    y, x = lax.axis_index("y"), lax.axis_index("x")
    place = y * RING + x
    seq = lax.axis_index(SEQ)
    starts = plane_starts(own // 2)

    positions = seq * seg + jnp.arange(seg, dtype=jnp.int32)
    current = doc_index(doc_starts, positions)
    one_back = (doc_index(doc_starts, positions - 1) == current).astype(f32)
    two_back = (doc_index(doc_starts, positions - 2) == current).astype(f32)

    channels = TPS * chans
    out_all = ring_gather(jnp.concatenate(ring_gather(out_weight, "x"), axis=0), "y")
    out_all = placed_blocks(out_all)
    in_wt = jnp.transpose(in_weight, (1, 2, 0))
    share = chans // 8
    taps_high = lax.reduce_precision(conv_taps, 8, 7)
    taps_mid = lax.reduce_precision(conv_taps - taps_high, 8, 7)
    taps_low = lax.reduce_precision(conv_taps - taps_high - taps_mid, 8, 7)
    taps_row = jnp.stack([taps_high, taps_mid, taps_low], axis=0).astype(bf16).reshape(1, 9 * chans)
    taps_row = jnp.pad(taps_row, ((0, share - 1), (0, width - 9 * chans)))
    in_share = lax.dynamic_slice_in_dim(in_wt, seq * share, share, axis=1)
    in_share = jnp.concatenate([in_share, taps_row[None]], axis=0)
    in_all = lax.all_gather(in_share, ALL, axis=0, tiled=False)
    in_all = in_all.reshape(8, TPS, 4, share, width)
    taps = in_all[0, :, 3, 0, : 9 * chans].astype(f32).reshape(TPS, 3, 3, chans)
    taps = (taps[:, 0] + taps[:, 1]) + taps[:, 2]
    taps = taps.transpose(1, 0, 2).reshape(3, channels)
    in_all = in_all[:, :, :3].transpose(2, 1, 0, 3, 4).reshape(3 * channels, width)

    flat_input = block_input.reshape(count, width)
    inverse_one = lax.rsqrt(jnp.mean(flat_input * flat_input, axis=-1, keepdims=True) + epsilon)
    normed1 = (flat_input * inverse_one * first_gain).astype(bf16)
    last = normed1.reshape(seqs, seg, width)[:, seg - 8 :]
    carried = lax.ppermute(
        last, ALL, [(i, i + TPS) for i in range(7 * TPS)]
    )
    in_flat = in_wt.reshape(3 * chans, width)
    mixer_blocks = []
    for s in range(seqs):
        proj = dot(in_flat, normed1[s * seg : (s + 1) * seg], 1, 1)
        edge = dot(in_flat, carried[s], 1, 1)
        product = (proj[:chans] * proj[2 * chans :]).astype(bf16)
        before = (edge[:chans] * edge[2 * chans :]).astype(bf16)
        extended = jnp.concatenate([before[:, 6:], product], axis=1).astype(f32)
        convolved = (
            conv_taps[0][:, None] * product.astype(f32)
            + conv_taps[1][:, None] * one_back[s] * extended[:, 1 : seg + 1]
            + conv_taps[2][:, None] * two_back[s] * extended[:, :seg]
        )
        mixed = (proj[chans : 2 * chans] * convolved).astype(bf16)
        mixer_blocks.append(mixed.reshape(chans, per_seq, own).transpose(1, 0, 2))
    mixer = lax.all_to_all(jnp.concatenate(mixer_blocks, axis=0), TP, 0, 0, tiled=True)
    mixer = mixer.reshape(channels, own)

    rows_in = lax.dynamic_slice_in_dim(flat_input, place * own, own, axis=0)
    residual = rows_in + dot(mixer, out_all, 0, 0)
    inverse_two = lax.rsqrt(jnp.mean(residual * residual, axis=-1, keepdims=True) + epsilon)
    normed2 = (residual * inverse_two * second_gain).astype(bf16)

    later = (normed2[0, 0].astype(f32) * 0.0).astype(jnp.int32)
    grad_low = relative_rows(out_cotangent.reshape(count, width), starts + later)
    both_t = jnp.concatenate([gate_weight.T, up_weight.T], axis=0)
    d_hidden = dot(grad_low, down_weight, 1, 1)

    def hidden_part(norms, d_hidden):
        both = dot(norms, both_t, 1, 1)
        gate, up = both[:, :ff], both[:, ff:]
        sig = jax.nn.sigmoid(gate)
        act = gate * sig
        hidden = (act * up).astype(bf16)
        d_gate = (d_hidden * up * sig * (1.0 + gate * (1.0 - sig))).astype(bf16)
        d_up = (d_hidden * act).astype(bf16)
        return jnp.concatenate([d_gate, d_up], axis=1), hidden

    def sums_part(d_both, hidden):
        return jnp.concatenate(
            [dot(d_both, both_t, 1, 0, bf16), dot(hidden, down_weight, 1, 0, bf16)], axis=1
        )

    norm_first, norm_last, in_all = plane_gather(normed2, in_all)
    norm_first = jnp.concatenate(norm_first, axis=0)
    norm_last = jnp.concatenate(norm_last, axis=0)
    split = norm_first.shape[0]
    both_first, hidden_first = hidden_part(norm_first, d_hidden[:split])
    both_last, hidden_last = hidden_part(norm_last, d_hidden[split:])
    sums_last = sums_part(both_last, hidden_last)
    sums_last, both_first, hidden_first = tied((sums_last, both_first, hidden_first))
    sums_first = sums_part(both_first, hidden_first)
    sums_first, both_last, hidden_last = tied((sums_first, both_last, hidden_last))
    ffn_grads = jnp.concatenate(
        [
            (dot(both_first, norm_first, 0, 0) + dot(both_last, norm_last, 0, 0)).astype(bf16),
            (
                dot(hidden_first, grad_low[:split], 0, 0)
                + dot(hidden_last, grad_low[split:], 0, 0)
            ).astype(bf16),
            jnp.zeros((32, width), bf16),
        ],
        axis=0,
    )
    ffn_grads = lax.psum_scatter(ffn_grads, SEQ, scatter_dimension=0, tiled=True)

    rows_n1 = lax.dynamic_slice_in_dim(normed1, place * own, own, axis=0)
    local_edge = lax.dynamic_slice_in_dim(normed1, place * own - 8, 8, axis=0)
    at_start = place % per_seq == 0
    edge_n1 = jnp.where(at_start, carried[place // per_seq], local_edge)
    again = dot(jnp.concatenate([edge_n1, rows_n1], axis=0), in_all, 1, 1)

    sums, (ffn_grads, again) = plane_scatter(sums_first, sums_last, (ffn_grads, again))
    d_normed2, ffn = sums[:, :width], sums[:, width:]
    ffn_grads = lax.all_gather(ffn_grads, SEQ, axis=0, tiled=True)
    gate_grad = ffn_grads[:ff].astype(f32).T
    up_grad = ffn_grads[ff : 2 * ff].astype(f32).T
    down_grad = ffn_grads[2 * ff : 3 * ff].astype(f32)

    block_output = lax.all_gather((residual + ffn).astype(bf16), TP, axis=0, tiled=True)
    block_output = block_output.astype(f32)

    grad_rows = lax.dynamic_slice_in_dim(
        out_cotangent.reshape(count, width), place * own, own, axis=0
    )
    scaled = second_gain * d_normed2
    second_part = jnp.sum(d_normed2 * residual * inverse_two, axis=0)
    d_residual = grad_rows + inverse_two * (
        scaled
        - residual
        * inverse_two
        * inverse_two
        * jnp.mean(scaled * residual, axis=-1, keepdims=True)
    )
    d_low = d_residual.astype(bf16)

    d_mixer = dot(d_low, out_all, 1, 1)

    b_all, c_all, x_all = (again[:, g * channels : (g + 1) * channels] for g in range(3))
    b_gate, c_gate, x_gate = b_all[8:], c_all[8:], x_all[8:]
    product = (b_all * x_all).astype(bf16).astype(f32)
    rows_one = lax.dynamic_slice_in_dim(one_back.reshape(count, 1), place * own, own, axis=0)
    rows_two = lax.dynamic_slice_in_dim(two_back.reshape(count, 1), place * own, own, axis=0)
    lagged_one = rows_one * product[7 : 7 + own]
    lagged_two = rows_two * product[6 : 6 + own]
    product = product[8:]
    convolved = taps[0] * product + taps[1] * lagged_one + taps[2] * lagged_two

    d_conv = d_mixer * c_gate
    d_cgate = d_mixer * convolved
    lag_one = rows_one * d_conv
    lag_two = rows_two * d_conv
    pairs = []
    for sq in range(8):
        for j in range(TPS):
            if j % per_seq:
                pairs.append((sq * TPS + j, sq * TPS + j - 1))
            elif sq:
                pairs.append((sq * TPS + j, (sq - 1) * TPS + j + per_seq - 1))
    edges = lax.ppermute(jnp.concatenate([lag_one[:2], lag_two[:2]], axis=0), ALL, pairs)
    ahead_one = jnp.concatenate([lag_one[1:], edges[:1]], axis=0)
    ahead_two = jnp.concatenate([lag_two[2:], edges[2:]], axis=0)
    d_product = taps[0] * d_conv + taps[1] * ahead_one + taps[2] * ahead_two
    d_projected = jnp.concatenate(
        [d_product * x_gate, d_cgate, d_product * b_gate], axis=1
    ).astype(bf16)
    d_normed1 = dot(d_projected, in_all, 1, 0)
    rows_inverse = lax.rsqrt(jnp.mean(rows_in * rows_in, axis=-1, keepdims=True) + epsilon)
    scaled_one = first_gain * d_normed1
    first_part = jnp.sum(d_normed1 * rows_in * rows_inverse, axis=0)
    input_rows = d_residual + rows_inverse * (
        scaled_one
        - rows_in
        * rows_inverse
        * rows_inverse
        * jnp.mean(scaled_one * rows_in, axis=-1, keepdims=True)
    )
    input_first, input_last, _ = plane_gather(input_rows.astype(bf16))
    input_grad = absolute_rows(input_first + input_last, starts)

    mixer_eighths = mixer.reshape(TPS, 8, chans // 8, own).transpose(1, 0, 2, 3)
    out_part = dot(mixer_eighths.reshape(channels, own), d_low, 1, 0, bf16)
    out_part = lax.psum_scatter(out_part, SEQ, scatter_dimension=0, tiled=True)
    out_part = out_part.reshape(TPS, chans // 8, width)
    is_low = lax.axis_index("core") == 0

    gains = jnp.stack([first_part, second_part], axis=0).astype(bf16)
    tap_sums = jnp.stack(
        [
            jnp.sum(d_conv * product, axis=0),
            jnp.sum(d_conv * lagged_one, axis=0),
            jnp.sum(d_conv * lagged_two, axis=0),
        ],
        axis=0,
    ).astype(bf16)
    tap_rows = tap_sums.reshape(3, TPS, chans).transpose(1, 0, 2).reshape(TPS, 1, 3 * chans)
    tap_rows = jnp.pad(tap_rows, ((0, 0), (0, 5), (0, width - 3 * chans)))
    gate_rows = d_projected.reshape(own, 3, TPS, chans).transpose(2, 1, 3, 0)
    rows = 3 * chans * own // width
    exchanged = jnp.concatenate(
        [
            gate_rows.reshape(TPS, rows, width),
            out_part,
            jnp.broadcast_to(gains[None], (TPS, 2, width)),
            tap_rows,
        ],
        axis=1,
    )
    exchanged = lax.all_to_all(exchanged, TP, 0, 0, tiled=True)
    received = exchanged[:, :rows].reshape(TPS, 3 * chans, own).transpose(1, 0, 2)
    in_part = dot(received.reshape(3 * chans, count), normed1, 1, 0, bf16)
    sums = jnp.sum(exchanged[:, rows:].astype(f32), axis=0).astype(bf16)

    middle = in_part.shape[0] // 2
    theirs = swap_cores(
        jnp.concatenate([jnp.where(is_low, in_part[middle:], in_part[:middle]), sums[8:]], axis=0)
    )
    mine = jnp.where(is_low, in_part[:middle], in_part[middle:])
    mine = jnp.concatenate([mine, sums[8:]], axis=0).astype(f32) + theirs.astype(f32)
    mine = jnp.concatenate([mine.astype(bf16), sums[:8]], axis=0)
    by_z = ring_gather(mine, "z")
    total = [part[: middle + 8].astype(f32) for part in by_z]
    total = (total[0] + total[2]) + (total[1] + total[3])
    out_rows = rolled(
        jnp.stack([part[middle + 8 :] for part in by_z], axis=0),
        0,
        (RING - lax.axis_index("z")) % RING,
    )
    small = total[middle:]
    mine = jnp.concatenate([total[:middle].astype(bf16), out_rows.reshape(RING * 8, width)], axis=0)
    theirs = swap_cores(mine)
    low, high = jnp.where(is_low, mine, theirs), jnp.where(is_low, theirs, mine)
    low, high = low.astype(f32), high.astype(f32)
    out_low, out_high = (part[middle:].reshape(RING, 1, 8, width) for part in (low, high))
    in_grad = jnp.concatenate([low[:middle], high[:middle]], axis=0)
    in_grad = in_grad.reshape(3, chans, width).transpose(2, 0, 1)
    out_grad = jnp.concatenate([out_low, out_high], axis=1).reshape(chans, width)
    first_grad, second_grad = small[0], small[1]
    taps_grad = small[2, : 3 * chans].reshape(3, chans)

    return (
        block_output.reshape(seqs, seg, width),
        input_grad.reshape(seqs, seg, width),
        first_grad,
        in_grad,
        taps_grad,
        out_grad,
        second_grad,
        gate_grad,
        up_grad,
        down_grad,
    )


def solution(mesh):
    grid = Mesh(mesh.devices.reshape(4, 2, RING, RING), ALL)
    return jax.shard_map(
        shards,
        mesh=grid,
        in_specs=(
            P(None, SEQ, None),
            P(),
            P(None, None, TP),
            P(None, TP),
            P(TP, None),
            P(),
            P(None, TP),
            P(None, TP),
            P(TP, None),
            P(),
            P(None, SEQ, None),
        ),
        out_specs=(
            P(None, SEQ, None),
            P(None, SEQ, None),
            P(),
            P(None, None, TP),
            P(None, TP),
            P(TP, None),
            P(),
            P(None, TP),
            P(None, TP),
            P(TP, None),
        ),
        check_vma=False,
    )
```

```python
import jax
import jax.numpy as jnp
from jax import lax
from jax.experimental import pallas as pl
from jax.experimental.pallas import tpu as pltpu
from jax.sharding import Mesh
from jax.sharding import PartitionSpec as P

epsilon = 1e-05
SEQ = ("z", "core")
TP = ("y", "x")
ALL = SEQ + TP
RING = 4
TPS = RING * RING
f32 = jnp.float32
bf16 = jnp.bfloat16


def turn(value, axis, steps):
    return lax.ppermute(value, axis, [(i, (i + steps) % RING) for i in range(RING)])


def ring_near(value, axis):
    return turn(value, axis, 3), turn(value, axis, 1)


def ring_far(near, axes):
    half = near[0].shape[0] // 2
    halves = assemble(
        near, (((1, 0, half),), ((0, half, half),), ((3, 0, half),), ((2, half, half),))
    )
    return tuple(turn(halves[i], axes[i // 2], (1, 3)[i % 2]) for i in range(4))


tied = lax.optimization_barrier


def plane_gather(value, early=(), launch=None, beside=()):
    half = value.shape[0] // 2
    top, bottom = assemble((value,), (((0, 0, half),), ((0, half, half),)))
    near = tuple(turn(top, "x", k) for k in (3, 2, 1)) + tuple(turn(bottom, "y", k) for k in (3, 2, 1))
    near, early = tied((near, early))
    launched, beside_last = launch(early) if launch else ((), ())
    top, bottom = assemble(
        (top, bottom) + near,
        (
            ((0, 0, half), (2, 0, half), (3, 0, half), (4, 0, half)),
            ((1, 0, half), (5, 0, half), (6, 0, half), (7, 0, half)),
        ),
    )
    near = ring_near(top, "y") + ring_near(bottom, "x")
    near, launched, beside = tied((near, launched, beside))
    far = ring_far(near, ("y", "x"))
    far, beside_last = tied((far, beside_last))
    return [top, near[0], near[1], bottom, near[2], near[3]], list(far), launched, beside_last, beside


def assemble(sources, plans):
    width, kind = sources[0].shape[1], sources[0].dtype
    copies = sum(len(plan) for plan in plans)

    def body(*refs):
        refs, sems = refs[:-1], refs[-1]
        started = []
        for out, plan in zip(refs[len(sources) :], plans):
            at = 0
            for source, start, rows in plan:
                copy = pltpu.make_async_copy(
                    refs[source].at[pl.ds(start, rows)],
                    out.at[pl.ds(at, rows)],
                    sems.at[len(started)],
                )
                copy.start()
                started.append(copy)
                at += rows
        for copy in started:
            copy.wait()

    shapes = [
        jax.ShapeDtypeStruct((sum(rows for _, _, rows in plan), width), kind) for plan in plans
    ]
    return pl.pallas_call(
        body,
        in_specs=[pl.BlockSpec(memory_space=pl.ANY)] * len(sources),
        out_specs=[pl.BlockSpec(memory_space=pl.ANY)] * len(plans),
        out_shape=shapes,
        scratch_shapes=[pltpu.SemaphoreType.DMA((copies,))],
        compiler_params=pltpu.CompilerParams(vmem_limit_bytes=2 * 1024 * 1024),
        cost_estimate=pl.CostEstimate(
            flops=0, bytes_accessed=4 * sum(x.size for x in shapes), transcendentals=0
        ),
        name="assemble",
    )(*sources)


def add_halves(blocks, moved):
    half, width = moved[0].shape
    count = len(blocks)

    def body(*refs):
        ins, more, outs = refs[:count], refs[count : 2 * count], refs[2 * count : 3 * count]
        held, added, in_sems, more_sems, out_sems = refs[3 * count :]

        def rows(ref, i):
            return ref.at[pl.ds(half * (i % 2), half)]

        loads = []
        for i in range(count):
            one = pltpu.make_async_copy(rows(ins[i], i), held.at[i], in_sems.at[i])
            two = pltpu.make_async_copy(more[i], added.at[i], more_sems.at[i])
            one.start()
            two.start()
            loads.append((one, two))
        stores = []
        for i in range(count):
            for load in loads[i]:
                load.wait()
            held[i] = (held[i].astype(f32) + added[i].astype(f32)).astype(bf16)
            store = pltpu.make_async_copy(held.at[i], rows(outs[i], i), out_sems.at[i])
            store.start()
            stores.append(store)
        for store in stores:
            store.wait()

    return pl.pallas_call(
        body,
        in_specs=[pl.BlockSpec(memory_space=pl.ANY)] * (2 * count),
        out_specs=[pl.BlockSpec(memory_space=pl.ANY)] * count,
        out_shape=[jax.ShapeDtypeStruct(x.shape, x.dtype) for x in blocks],
        input_output_aliases={i: i for i in range(count)},
        scratch_shapes=[
            pltpu.VMEM((count, half, width), bf16),
            pltpu.VMEM((count, half, width), bf16),
            pltpu.SemaphoreType.DMA((count,)),
            pltpu.SemaphoreType.DMA((count,)),
            pltpu.SemaphoreType.DMA((count,)),
        ],
        compiler_params=pltpu.CompilerParams(vmem_limit_bytes=8 * 1024 * 1024),
        cost_estimate=pl.CostEstimate(
            flops=count * half * width, bytes_accessed=6 * count * half * width, transcendentals=0
        ),
        name="add_halves",
    )(*blocks, *moved)


def scatter_far(pieces, axes):
    return tied(
        tuple(turn(pieces[i], axes[i // 2], (1, 3)[i % 2]) for i in range(4))
    )


def scatter_near(blocks, moved, axes):
    blocks = add_halves(blocks, moved)
    return tuple(turn(blocks[i], axes[i // 2], (1, 3)[i % 2]) for i in range(4))


def in_vmem(count):
    return [pl.BlockSpec(memory_space=pltpu.VMEM)] * count


def whole(*shapes):
    return [
        pl.BlockSpec(
            shape, lambda *_, rank=len(shape): (0,) * rank, pipeline_mode=pl.Buffered(buffer_count=1)
        )
        for shape in shapes
    ]


def hbm_call(body, operands, outs, megabytes, flops, name):
    def outer(*refs):
        n, m = len(operands), len(outs)
        held, held_outs = refs[n + m : 2 * n + m], refs[2 * n + m : 2 * n + 2 * m]
        sems = refs[-1]
        loads = [pltpu.make_async_copy(refs[i], held[i], sems.at[i]) for i in range(n)]
        for load in loads:
            load.start()
        for load in loads:
            load.wait()
        body(*held, *held_outs)
        stores = [
            pltpu.make_async_copy(held_outs[i], refs[n + i], sems.at[n + i]) for i in range(m)
        ]
        for store in stores:
            store.start()
        for store in stores:
            store.wait()

    arrays = list(operands) + list(outs)
    return pl.pallas_call(
        outer,
        in_specs=[pl.BlockSpec(memory_space=pltpu.HBM)] * len(operands),
        out_specs=[pl.BlockSpec(memory_space=pltpu.HBM)] * len(outs),
        out_shape=list(outs),
        scratch_shapes=[pltpu.VMEM(x.shape, x.dtype) for x in arrays]
        + [pltpu.SemaphoreType.DMA((len(arrays),))],
        compiler_params=pltpu.CompilerParams(vmem_limit_bytes=megabytes * 1024 * 1024),
        cost_estimate=pl.CostEstimate(
            flops=flops,
            bytes_accessed=sum(x.size * x.dtype.itemsize for x in arrays),
            transcendentals=0,
        ),
        name=name,
    )(*operands)


def ring_sums(own, one, other):
    rows, width = own.shape
    step = rows // RING
    cuts = tuple(step * k for k in range(RING + 1))

    def body(own_ref, one_ref, other_ref, *outs):
        for out, low, high in zip(outs, cuts[:-1], cuts[1:]):
            total = own_ref[low:high, :].astype(f32) + (
                one_ref[low:high, :].astype(f32) + other_ref[low:high, :].astype(f32)
            )
            out[...] = total.astype(out.dtype)

    return pl.pallas_call(
        body,
        grid=(1,),
        in_specs=whole(*[own.shape] * 3),
        out_specs=whole(*((high - low, width) for low, high in zip(cuts[:-1], cuts[1:]))),
        out_shape=[
            jax.ShapeDtypeStruct((high - low, width), f32 if low == 0 else bf16)
            for low, high in zip(cuts[:-1], cuts[1:])
        ],
        compiler_params=pltpu.CompilerParams(vmem_limit_bytes=10 * 1024 * 1024),
        cost_estimate=pl.CostEstimate(
            flops=2 * rows * width, bytes_accessed=8 * rows * width, transcendentals=0
        ),
        name="ring_sums",
    )(own, one, other)


def swap_cores(value):
    return lax.ppermute(value, "core", [(0, 1), (1, 0)])


CHUNKS = ((0, 0), (0, 1), (0, 3), (1, 0), (1, 1), (1, 3), (0, 2), (1, 2))


def plane_starts(half):
    y, x = lax.axis_index("y"), lax.axis_index("x")
    side = jnp.array([s for s, _ in CHUNKS for _ in range(RING)], jnp.int32)
    outer = jnp.array([k for _, k in CHUNKS for _ in range(RING)], jnp.int32)
    inner = jnp.array([k for _ in CHUNKS for k in range(RING)], jnp.int32)
    row = (jnp.where(side == 0, outer, inner) + y) % RING
    column = (jnp.where(side == 0, inner, outer) + x) % RING
    return (2 * (row * RING + column) + side) * half


def relative_rows(rows, starts, weight, split):
    half, width = rows.shape[0] // TPS // 2, rows.shape[1]
    count, units = rows.shape[0], weight.shape[0]
    slots = 8

    def body(table, source, weight_ref, low_a, low_b, hidden_a, hidden_b, held, lows, hiddens, *sems):
        sems, low_sems, hidden_sems = sems
        def copy(i):
            start = pl.multiple_of(table[i], half)
            return pltpu.make_async_copy(
                source.at[pl.ds(start, half)], held.at[i % slots], sems.at[i % slots]
            )

        for i in range(slots):
            copy(i).start()
        outs = []
        for i in range(0, 2 * TPS, RING):
            parts = []
            for j in range(i, i + RING):
                copy(j).wait()
                parts.append(held[j % slots].astype(bf16))
            low = jnp.concatenate(parts, axis=0)
            for j in range(i + slots, min(i + slots + RING, 2 * TPS)):
                copy(j).start()
            at, k = i * half, i // RING
            to_low, to_hidden = (low_a, hidden_a) if at < split else (low_b, hidden_b)
            at = at if at < split else at - split
            lows[k] = low
            hiddens[k] = dot(low, weight_ref[...], 1, 1)
            rows = pl.ds(at, RING * half)
            out = pltpu.make_async_copy(lows.at[k], to_low.at[rows], low_sems.at[k])
            out.start()
            outs.append(out)
            out = pltpu.make_async_copy(hiddens.at[k], to_hidden.at[rows], hidden_sems.at[k])
            out.start()
            outs.append(out)
        for out in outs:
            out.wait()

    return pl.pallas_call(
        body,
        grid_spec=pltpu.PrefetchScalarGridSpec(
            num_scalar_prefetch=1,
            grid=(1,),
            in_specs=[
                pl.BlockSpec(memory_space=pltpu.HBM),
                pl.BlockSpec(memory_space=pltpu.VMEM),
            ],
            out_specs=[pl.BlockSpec(memory_space=pltpu.HBM)] * 4,
            scratch_shapes=[
                pltpu.VMEM((slots, half, width), f32),
                pltpu.VMEM((2 * TPS // RING, RING * half, width), bf16),
                pltpu.VMEM((2 * TPS // RING, RING * half, units), f32),
                pltpu.SemaphoreType.DMA((slots,)),
                pltpu.SemaphoreType.DMA((2 * TPS // RING,)),
                pltpu.SemaphoreType.DMA((2 * TPS // RING,)),
            ],
        ),
        out_shape=[
            jax.ShapeDtypeStruct((split, width), bf16),
            jax.ShapeDtypeStruct((count - split, width), bf16),
            jax.ShapeDtypeStruct((split, units), f32),
            jax.ShapeDtypeStruct((count - split, units), f32),
        ],
        compiler_params=pltpu.CompilerParams(vmem_limit_bytes=16 * 1024 * 1024),
        cost_estimate=pl.CostEstimate(
            flops=2 * rows.size * units, bytes_accessed=rows.size * 6, transcendentals=0
        ),
        name="relative_rows",
    )(starts, rows, weight)


def absolute_rows(chunks, starts):
    total, width = sum(chunk.shape[0] for chunk in chunks), chunks[0].shape[1]
    half = total // TPS // 2
    slots = 16
    pieces = [(k, j) for k, chunk in enumerate(chunks) for j in range(chunk.shape[0] // half)]

    def body(table, *refs):
        parts, out, held, sems = refs[: len(chunks)], refs[-3], refs[-2], refs[-1]

        def copy(i):
            start = pl.multiple_of(table[i], half)
            return pltpu.make_async_copy(
                held.at[i % slots], out.at[pl.ds(start, half)], sems.at[i % slots]
            )

        for i, (k, j) in enumerate(pieces):
            if i >= slots:
                copy(i - slots).wait()
            held[i % slots] = parts[k][j * half : (j + 1) * half, :].astype(f32)
            copy(i).start()
        for i in range(2 * TPS - slots, 2 * TPS):
            copy(i).wait()

    return pl.pallas_call(
        body,
        grid_spec=pltpu.PrefetchScalarGridSpec(
            num_scalar_prefetch=1,
            grid=(1,),
            in_specs=[pl.BlockSpec(memory_space=pltpu.VMEM)] * len(chunks),
            out_specs=pl.BlockSpec(memory_space=pl.ANY),
            scratch_shapes=[
                pltpu.VMEM((slots, half, width), f32),
                pltpu.SemaphoreType.DMA((slots,)),
            ],
        ),
        out_shape=jax.ShapeDtypeStruct((total, width), f32),
        compiler_params=pltpu.CompilerParams(vmem_limit_bytes=7 * 1024 * 1024),
        cost_estimate=pl.CostEstimate(
            flops=total * width, bytes_accessed=total * width * 6, transcendentals=0
        ),
        name="absolute_rows",
    )(starts, *chunks)


def norm_and_project(rows, gain, weight):
    count, width = rows.shape
    chans = weight.shape[0]
    step = 256

    def body(rows_ref, gain_ref, weight_ref, normed_ref, out_ref):
        block = rows_ref[...]
        inverse = lax.rsqrt(jnp.mean(block * block, axis=-1, keepdims=True) + epsilon)
        normed = (block * inverse * gain_ref[...]).astype(bf16)
        normed_ref[...] = normed
        out_ref[...] = dot(weight_ref[...], normed, 1, 1)

    return pl.pallas_call(
        body,
        grid=(count // step,),
        in_specs=[
            pl.BlockSpec((step, width), lambda i: (i, 0)),
            pl.BlockSpec((1, width), lambda i: (0, 0)),
            pl.BlockSpec((chans, width), lambda i: (0, 0)),
        ],
        out_specs=[
            pl.BlockSpec((step, width), lambda i: (i, 0)),
            pl.BlockSpec((chans, step), lambda i: (0, i)),
        ],
        out_shape=[
            jax.ShapeDtypeStruct((count, width), bf16),
            jax.ShapeDtypeStruct((chans, count), f32),
        ],
        compiler_params=pltpu.CompilerParams(vmem_limit_bytes=6 * 1024 * 1024),
        cost_estimate=pl.CostEstimate(
            flops=2 * count * width * chans, bytes_accessed=6 * count * width, transcendentals=0
        ),
        name="norm_and_project",
    )(rows, gain.reshape(1, width), weight)


def mixer_gates(rows, weight, taps, mask_one, mask_two):
    own, width = mask_one.shape[0], rows.shape[1]
    chans = taps.shape[1]

    def body(rows_ref, weight_ref, taps_ref, one_ref, two_ref, gates_ref, lags_ref, conv_ref):
        b_gate = dot(rows_ref[...], weight_ref[:chans, :], 1, 1)
        c_gate = dot(rows_ref[8:, :], weight_ref[chans : 2 * chans, :], 1, 1)
        x_gate = dot(rows_ref[...], weight_ref[2 * chans :, :], 1, 1)
        product = (b_gate * x_gate).astype(bf16).astype(f32)
        one = one_ref[...] * product[7 : 7 + own]
        two = two_ref[...] * product[6 : 6 + own]
        product = product[8:]
        gates_ref[0] = b_gate[8:]
        gates_ref[1] = c_gate
        gates_ref[2] = x_gate[8:]
        lags_ref[0] = product
        lags_ref[1] = one
        lags_ref[2] = two
        conv_ref[...] = taps_ref[0:1, :] * product + taps_ref[1:2, :] * one + taps_ref[2:3, :] * two

    operands = (rows, weight, taps, mask_one, mask_two)
    outs = [
        jax.ShapeDtypeStruct((3, own, chans), f32),
        jax.ShapeDtypeStruct((3, own, chans), f32),
        jax.ShapeDtypeStruct((own, chans), f32),
    ]
    return pl.pallas_call(
        body,
        grid=(1,),
        in_specs=whole(*(x.shape for x in operands)),
        out_specs=whole(*(x.shape for x in outs)),
        out_shape=outs,
        compiler_params=pltpu.CompilerParams(vmem_limit_bytes=28 * 1024 * 1024),
        cost_estimate=pl.CostEstimate(
            flops=6 * own * width * chans, bytes_accessed=6 * width * chans, transcendentals=0
        ),
        name="mixer_gates",
    )(*operands)


def residual_back(own_sums, moved, residual, inverse, gain, grad, weight, c_rows, mask_one, mask_two):
    own, width = residual.shape
    half = own // 2
    chans = weight.shape[0]

    def body(*refs):
        sums, moved_refs, refs = refs[:2], refs[2:8], refs[8:]
        res_ref, inv_ref, gain_ref, grad_ref, weight_ref, gates_ref, one_ref, two_ref = refs[:8]
        block_ref, d_res_ref, low_ref, part_ref, mixer_ref, edge_ref = refs[8:]
        parts = []
        for i in range(2):
            rows = slice(i * half, (i + 1) * half)
            total = sums[i][...]
            for part in moved_refs[3 * i : 3 * i + 3]:
                total = total + part[...].astype(f32)
            d_norm, ffn = total[:, :width], total[:, width:]
            res, inv = res_ref[rows, :], inv_ref[rows, :]
            block_ref[rows, :] = (res + ffn).astype(bf16)
            parts.append(jnp.sum(d_norm * res * inv, axis=0, keepdims=True))
            scaled = gain_ref[...] * d_norm
            mean = jnp.mean(scaled * res, axis=-1, keepdims=True)
            d_res = grad_ref[rows, :] + inv * (scaled - res * inv * inv * mean)
            d_res_ref[rows, :] = d_res
            low_ref[rows, :] = d_res.astype(bf16)
        part_ref[...] = parts[0] + parts[1]
        d_mixer = dot(low_ref[...], weight_ref[...], 1, 1)
        mixer_ref[...] = d_mixer
        d_conv = d_mixer[:8] * gates_ref[...]
        edge_ref[0:8, :] = one_ref[:8, :] * d_conv
        edge_ref[8:16, :] = two_ref[:8, :] * d_conv

    operands = (*own_sums, *moved, residual, inverse, gain, grad, weight, c_rows, mask_one, mask_two)
    outs = [
        jax.ShapeDtypeStruct((own, width), bf16),
        jax.ShapeDtypeStruct((own, width), f32),
        jax.ShapeDtypeStruct((own, width), bf16),
        jax.ShapeDtypeStruct((1, width), f32),
        jax.ShapeDtypeStruct((own, chans), f32),
        jax.ShapeDtypeStruct((16, chans), f32),
    ]
    return hbm_call(body, operands, outs, 60, 2 * own * width * chans, "residual_back")


def mixer_back(
    d_mixer, edges, gates, lags, conv, mask_one, mask_two, taps, weight, rows, gain, d_res, second, halves
):
    own, width = rows.shape
    chans = d_mixer.shape[1]
    per = chans // TPS
    extra = 2 * width // own + 8

    def body(*refs):
        mixer_ref, edge_ref, gates_ref, lags_ref, conv_ref, one_ref, two_ref = refs[:7]
        taps_ref, weight_ref, rows_ref, gain_ref, d_res_ref, second_ref, halves_ref = refs[7:14]
        out_ref, send_ref, grads_ref = refs[14:]
        d_mix = mixer_ref[...]
        d_conv = d_mix * gates_ref[1]
        lag_one = one_ref[...] * d_conv
        lag_two = two_ref[...] * d_conv
        ahead_one = jnp.concatenate([lag_one[1:], edge_ref[0:1, :]], axis=0)
        ahead_two = jnp.concatenate([lag_two[2:], edge_ref[8:10, :]], axis=0)
        d_product = (
            taps_ref[0:1, :] * d_conv + taps_ref[1:2, :] * ahead_one + taps_ref[2:3, :] * ahead_two
        )
        grads_ref[0] = (d_product * gates_ref[2]).astype(bf16)
        grads_ref[1] = (d_mix * conv_ref[...]).astype(bf16)
        grads_ref[2] = (d_product * gates_ref[0]).astype(bf16)
        d_norm = dot(grads_ref[0], weight_ref[:chans, :], 1, 0)
        d_norm = d_norm + dot(grads_ref[1], weight_ref[chans : 2 * chans, :], 1, 0)
        d_norm = d_norm + dot(grads_ref[2], weight_ref[2 * chans :, :], 1, 0)
        block = rows_ref[...]
        inverse = lax.rsqrt(jnp.mean(block * block, axis=-1, keepdims=True) + epsilon)
        first = jnp.sum(d_norm * block * inverse, axis=0, keepdims=True)
        scaled = gain_ref[...] * d_norm
        mean = jnp.mean(scaled * block, axis=-1, keepdims=True)
        out = d_res_ref[...] + inverse * (scaled - block * inverse * inverse * mean)
        out_ref[...] = out.astype(bf16)
        tap_sums = [jnp.sum(d_conv * lags_ref[k], axis=0, keepdims=True) for k in range(3)]
        sums = jnp.concatenate(tap_sums + [jnp.zeros((5, chans), f32)], axis=0)
        gains = []
        for value in (first, second_ref[...]):
            gains += [value[:, k * own : (k + 1) * own] for k in range(width // own)]
        gains = jnp.concatenate(gains, axis=0)
        for g in range(3):
            turned = grads_ref[g].astype(f32).T.astype(bf16)
            for j in range(TPS):
                send_ref[j, g * per : (g + 1) * per, :] = turned[j * per : (j + 1) * per]
        for j in range(TPS):
            pair = j // 2 * 2 * per
            tail = jnp.concatenate([gains, sums[:, pair : pair + 2 * per]], axis=0)
            send_ref[j, 3 * per : 3 * per + extra, :] = tail.astype(bf16)
            for k in range(width // own):
                at = 3 * per + extra + k * halves.shape[1]
                send_ref[j, at : at + halves.shape[1], :] = halves_ref[j, :, k * own : (k + 1) * own]

    operands = (d_mixer, edges, gates, lags, conv, mask_one, mask_two, taps, weight, rows, gain, d_res, second, halves)
    outs = [
        jax.ShapeDtypeStruct((own, width), bf16),
        jax.ShapeDtypeStruct((TPS, 3 * per + extra + halves.shape[1] * width // own, own), bf16),
    ]
    return pl.pallas_call(
        body,
        grid=(1,),
        in_specs=whole(*(x.shape for x in operands)),
        out_specs=whole(*(x.shape for x in outs)),
        out_shape=outs,
        scratch_shapes=[pltpu.VMEM((3, own, chans), bf16)],
        compiler_params=pltpu.CompilerParams(vmem_limit_bytes=36 * 1024 * 1024),
        cost_estimate=pl.CostEstimate(
            flops=6 * own * width * chans, bytes_accessed=6 * width * chans, transcendentals=0
        ),
        name="mixer_back",
    )(*operands)


def feed_forward(norms, d_hidden, gate_t, up_t, down, pieces):
    count, ff = d_hidden.shape
    width = down.shape[1]
    step = norms[0].shape[0]
    piece = count // pieces

    def body(*refs):
        norm_refs, rest = refs[: len(norms)], refs[len(norms) :]
        d_hbm, gate_ref, up_ref, down_ref = rest[:4]
        outs, (d_gate_ref, d_up_ref, hidden_ref, d_ref, sem) = rest[4:-5], rest[-5:]
        load = pltpu.make_async_copy(d_hbm, d_ref, sem)
        load.start()
        for k, norm_ref in enumerate(norm_refs):
            part = slice(k * step, (k + 1) * step)
            norm = norm_ref[...]
            gate = dot(norm, gate_ref[...], 1, 1)
            up = dot(norm, up_ref[...], 1, 1)
            if k == 0:
                load.wait()
            d_part = d_ref[part, :]
            sig = jax.nn.sigmoid(gate)
            act = gate * sig
            hidden = (act * up).astype(bf16)
            d_gate = (d_part * up * sig * (1.0 + gate * (1.0 - sig))).astype(bf16)
            d_up = (d_part * act).astype(bf16)
            d_gate_ref[part, :] = d_gate
            d_up_ref[part, :] = d_up
            hidden_ref[part, :] = hidden
            d_norm = (dot(d_gate, gate_ref[...], 1, 0) + dot(d_up, up_ref[...], 1, 0)).astype(bf16)
            ffn = dot(hidden, down_ref[...], 1, 0, bf16)
            first = k * step // piece
            for j in range(max(1, step // piece)):
                inside = slice(j * piece, (j + 1) * piece)
                outs[first + j][:, :width] = d_norm[inside]
                outs[first + j][:, width:] = ffn[inside]

    outs = pl.pallas_call(
        body,
        in_specs=in_vmem(len(norms)) + [pl.BlockSpec(memory_space=pltpu.HBM)] + in_vmem(3),
        out_specs=in_vmem(pieces + 3),
        out_shape=[jax.ShapeDtypeStruct((piece, 2 * width), bf16)] * pieces
        + [jax.ShapeDtypeStruct((count, ff), bf16)] * 3,
        scratch_shapes=[pltpu.VMEM(d_hidden.shape, f32), pltpu.SemaphoreType.DMA(())],
        compiler_params=pltpu.CompilerParams(vmem_limit_bytes=12 * 1024 * 1024),
        cost_estimate=pl.CostEstimate(
            flops=10 * count * width * ff,
            bytes_accessed=count * width * 6,
            transcendentals=count * ff,
        ),
        name="feed_forward",
    )(*norms, d_hidden, gate_t, up_t, down)
    return outs[:pieces], outs[pieces:]


def dot(left, right, left_dim, right_dim, kind=f32):
    out = lax.dot_general(
        left, right, (((left_dim,), (right_dim,)), ((), ())), preferred_element_type=f32
    )
    return out.astype(kind)


def doc_index(doc_starts, positions):
    hits = (doc_starts[:, None, :] <= positions[None, :, None]).astype(jnp.int32)
    return jnp.sum(hits, axis=-1) - 1


def shards(
    block_input,
    first_gain,
    in_weight,
    conv_taps,
    out_weight,
    second_gain,
    gate_weight,
    up_weight,
    down_weight,
    doc_starts,
    out_cotangent,
):
    seqs, seg, width = block_input.shape
    chans = in_weight.shape[2]
    ff = gate_weight.shape[1]
    count = seqs * seg
    own = count // TPS
    per_seq = TPS // seqs
    y, x = lax.axis_index("y"), lax.axis_index("x")
    place = y * RING + x
    seq = lax.axis_index(SEQ)
    starts = plane_starts(own // 2)

    positions = seq * seg + jnp.arange(seg, dtype=jnp.int32)
    current = doc_index(doc_starts, positions)
    one_back = (doc_index(doc_starts, positions - 1) == current).astype(f32)
    two_back = (doc_index(doc_starts, positions - 2) == current).astype(f32)

    channels = TPS * chans
    is_low = lax.axis_index("core") == 0
    out_half = lax.dynamic_slice_in_dim(
        out_weight, lax.axis_index("core") * (chans // 2), chans // 2, axis=0
    )
    out_mine = jnp.broadcast_to(out_half[None], (TPS, chans // 2, width))
    out_mine = lax.all_to_all(out_mine, TP, 0, 0, tiled=True)
    out_theirs = swap_cores(out_mine)
    out_all = jnp.stack(
        [jnp.where(is_low, out_mine, out_theirs), jnp.where(is_low, out_theirs, out_mine)], axis=1
    ).reshape(channels, width)
    in_wt = jnp.transpose(in_weight, (1, 2, 0))
    share = chans // 8
    taps_high = lax.reduce_precision(conv_taps, 8, 7)
    taps_mid = lax.reduce_precision(conv_taps - taps_high, 8, 7)
    taps_low = lax.reduce_precision(conv_taps - taps_high - taps_mid, 8, 7)
    taps_row = jnp.stack([taps_high, taps_mid, taps_low], axis=0).astype(bf16).reshape(1, 9 * chans)
    taps_row = jnp.pad(taps_row, ((0, share - 1), (0, width - 9 * chans)))
    in_share = lax.dynamic_slice_in_dim(in_wt, seq * share, share, axis=1)
    in_share = jnp.concatenate([in_share, taps_row[None]], axis=0)
    in_all = lax.all_gather(in_share, ALL, axis=0, tiled=False)
    in_all = in_all.reshape(8, TPS, 4, share, width)
    taps = in_all[0, :, 3, 0, : 9 * chans].astype(f32).reshape(TPS, 3, 3, chans)
    taps = (taps[:, 0] + taps[:, 1]) + taps[:, 2]
    taps = taps.transpose(1, 0, 2).reshape(3, channels)
    in_all = in_all[:, :, :3].transpose(2, 1, 0, 3, 4).reshape(3 * channels, width)

    flat_input = block_input.reshape(count, width)
    in_flat = in_wt.reshape(3 * chans, width)
    normed1, projected = norm_and_project(flat_input, first_gain, in_flat)
    last = normed1.reshape(seqs, seg, width)[:, seg - 8 :]
    carried = lax.ppermute(
        last, ALL, [(i, i + TPS) for i in range(7 * TPS)]
    )
    mixer_blocks = []
    for s in range(seqs):
        proj = projected[:, s * seg : (s + 1) * seg]
        edge = dot(in_flat, carried[s], 1, 1)
        product = (proj[:chans] * proj[2 * chans :]).astype(bf16)
        before = (edge[:chans] * edge[2 * chans :]).astype(bf16)
        extended = jnp.concatenate([before[:, 6:], product], axis=1).astype(f32)
        convolved = (
            conv_taps[0][:, None] * product.astype(f32)
            + conv_taps[1][:, None] * one_back[s] * extended[:, 1 : seg + 1]
            + conv_taps[2][:, None] * two_back[s] * extended[:, :seg]
        )
        mixed = (proj[chans : 2 * chans] * convolved).astype(bf16)
        mixer_blocks.append(mixed.reshape(chans, per_seq, own).transpose(1, 0, 2))
    mixer_blocks = jnp.concatenate(mixer_blocks, axis=0)
    later = (mixer_blocks[0, 0, 0].astype(f32) * 0.0).astype(jnp.int32)
    split = count * 3 // 4
    *grad_low, hidden_first, hidden_last = relative_rows(
        out_cotangent.reshape(count, width), starts + later, down_weight, split
    )
    mixer = lax.all_to_all(mixer_blocks, TP, 0, 0, tiled=True)
    mixer, hidden_first, hidden_last = tied((mixer, hidden_first, hidden_last))
    mixer = mixer.reshape(channels, own)

    rows_in = lax.dynamic_slice_in_dim(flat_input, place * own, own, axis=0)
    residual = rows_in + dot(mixer, out_all, 0, 0)
    inverse_two = lax.rsqrt(jnp.mean(residual * residual, axis=-1, keepdims=True) + epsilon)
    normed2 = (residual * inverse_two * second_gain).astype(bf16)

    gate_t, up_t = gate_weight.T, up_weight.T
    norm_first, norm_last, _, _, in_all = plane_gather(normed2, beside=in_all)
    sums_first, kept_first = feed_forward(
        norm_first, hidden_first, gate_t, up_t, down_weight, 6
    )
    piece = norm_last[0].shape[0]
    norm_last = assemble(
        norm_last, (((0, 0, piece), (1, 0, piece)), ((2, 0, piece), (3, 0, piece)))
    )
    norm_last, sums_first = tied((norm_last, sums_first))
    sums_last, kept_last = feed_forward(norm_last, hidden_last, gate_t, up_t, down_weight, 4)
    moved = scatter_far(sums_last, ("y", "x"))
    moved, kept_first, kept_last, norm_first, norm_last = tied(
        (moved, kept_first, kept_last, norm_first, norm_last)
    )
    rows = norm_last[0].shape[0]
    norm_first, norm_last = assemble(
        tuple(norm_first) + tuple(norm_last),
        (tuple((i, 0, rows) for i in range(6)), ((6, 0, rows), (7, 0, rows))),
    )
    ffn_grads = []
    for k in range(3):
        right_first = norm_first if k < 2 else grad_low[0]
        right_last = norm_last if k < 2 else grad_low[1]
        part = dot(kept_first[k], right_first, 0, 0) + dot(kept_last[k], right_last, 0, 0)
        ffn_grads.append(part.astype(bf16))
    ffn_grads = jnp.concatenate(ffn_grads + [jnp.zeros((32, width), bf16)], axis=0)
    ffn_grads = lax.psum_scatter(ffn_grads, SEQ, scatter_dimension=0, tiled=True)

    rows_n1 = lax.dynamic_slice_in_dim(normed1, place * own, own, axis=0)
    local_edge = lax.dynamic_slice_in_dim(normed1, place * own - 8, 8, axis=0)
    at_start = place % per_seq == 0
    edge_n1 = jnp.where(at_start, carried[place // per_seq], local_edge)
    rows_one = lax.dynamic_slice_in_dim(one_back.reshape(count, 1), place * own, own, axis=0)
    rows_two = lax.dynamic_slice_in_dim(two_back.reshape(count, 1), place * own, own, axis=0)
    rows_n1 = jnp.concatenate([edge_n1, rows_n1], axis=0)

    moved = scatter_near([sums_first[i] for i in (1, 2, 4, 5)], moved, ("y", "x"))
    gates, lags, conv = mixer_gates(rows_n1, in_all, taps, rows_one, rows_two)
    moved, gates, lags, conv = tied((moved, gates, lags, conv))
    top = ring_sums(sums_first[0], *moved[:2])
    bottom = ring_sums(sums_first[3], *moved[2:])
    moved = tuple(turn(top[k], "x", k) for k in (1, 2, 3))
    moved = moved + tuple(turn(bottom[k], "y", k) for k in (1, 2, 3))
    moved, ffn_grads = tied((moved, ffn_grads))

    grad_rows = lax.dynamic_slice_in_dim(
        out_cotangent.reshape(count, width), place * own, own, axis=0
    )
    block_rows, d_residual, d_low, second_part, d_mixer, edges = residual_back(
        (top[0], bottom[0]),
        moved,
        residual,
        inverse_two,
        second_gain.reshape(1, width),
        grad_rows,
        out_all,
        gates[1, :8],
        rows_one,
        rows_two,
    )
    block_output = lax.all_gather(block_rows, TP, axis=0, tiled=True)
    pairs = []
    for sq in range(8):
        for j in range(TPS):
            if j % per_seq:
                pairs.append((sq * TPS + j, sq * TPS + j - 1))
            elif sq:
                pairs.append((sq * TPS + j, (sq - 1) * TPS + j + per_seq - 1))
    edges = lax.ppermute(edges, ALL, pairs)
    out_part = dot(mixer, d_low, 1, 0, bf16).reshape(TPS, 2, chans // 2, width)
    theirs = swap_cores(jnp.where(is_low, out_part[:, 1], out_part[:, 0]))
    out_part = jnp.where(is_low, out_part[:, 0], out_part[:, 1]).astype(f32) + theirs.astype(f32)
    input_rows, exchanged = mixer_back(
        d_mixer,
        edges,
        gates,
        lags,
        conv,
        rows_one,
        rows_two,
        taps,
        in_all,
        rows_in,
        first_gain.reshape(1, width),
        d_residual,
        second_part,
        out_part.astype(bf16),
    )
    middle = 3 * chans // 2

    def exchange(early):
        exchanged, ffn_grads = early
        exchanged = lax.all_to_all(exchanged, TP, 0, 0, tiled=True)
        return exchanged, lax.all_gather(ffn_grads, SEQ, axis=0, tiled=True)

    input_first, input_last, exchanged, ffn_grads, block_output = plane_gather(
        input_rows, (exchanged, ffn_grads), exchange, block_output
    )
    received = exchanged[:, : 3 * chans].transpose(1, 0, 2)
    in_part = dot(received.reshape(3 * chans, count), normed1, 1, 0, bf16)
    small = jnp.sum(exchanged[:, 3 * chans :].astype(f32), axis=0).astype(bf16)
    out_part = small[24:].reshape(width // own, chans // 2, own).transpose(1, 0, 2)
    out_part = out_part.reshape(chans // 2, width)
    small = jnp.pad(small[:24].reshape(3, width), ((0, 5), (0, 0)))
    theirs = swap_cores(
        jnp.concatenate([jnp.where(is_low, in_part[middle:], in_part[:middle]), small], axis=0)
    )
    mine = jnp.where(is_low, in_part[:middle], in_part[middle:])
    mine = jnp.concatenate([mine, small], axis=0).astype(f32) + theirs.astype(f32)
    mine = jnp.concatenate([mine.astype(bf16), out_part], axis=0)
    by_z = jnp.broadcast_to(mine[None], (RING,) + mine.shape)
    by_z = lax.all_to_all(by_z, "z", 0, 0, tiled=True)
    block_output = block_output.astype(f32)
    gate_grad = ffn_grads[:ff].astype(f32).T
    up_grad = ffn_grads[ff : 2 * ff].astype(f32).T
    down_grad = ffn_grads[2 * ff : 3 * ff].astype(f32)
    input_grad = absolute_rows(input_first + input_last, starts)

    by_z = by_z.astype(f32)
    total = (by_z[0] + by_z[2]) + (by_z[1] + by_z[3])
    small = total[middle : middle + 8]
    mine = jnp.concatenate([total[:middle], total[middle + 8 :]], axis=0).astype(bf16)
    theirs = swap_cores(mine)
    low, high = jnp.where(is_low, mine, theirs), jnp.where(is_low, theirs, mine)
    low, high = low.astype(f32), high.astype(f32)
    in_grad = jnp.concatenate([low[:middle], high[:middle]], axis=0)
    in_grad = in_grad.reshape(3, chans, width).transpose(2, 0, 1)
    out_grad = jnp.concatenate([low[middle:], high[middle:]], axis=0)
    first_grad, second_grad = small[0], small[1]
    taps_grad = small[2].reshape(8, own)[:3]
    taps_grad = lax.dynamic_slice_in_dim(taps_grad, place % 2 * chans, chans, axis=1)

    return (
        block_output.reshape(seqs, seg, width),
        input_grad.reshape(seqs, seg, width),
        first_grad,
        in_grad,
        taps_grad,
        out_grad,
        second_grad,
        gate_grad,
        up_grad,
        down_grad,
    )


def solution(mesh):
    grid = Mesh(mesh.devices.reshape(4, 2, RING, RING), ALL)
    return jax.shard_map(
        shards,
        mesh=grid,
        in_specs=(
            P(None, SEQ, None),
            P(),
            P(None, None, TP),
            P(None, TP),
            P(TP, None),
            P(),
            P(None, TP),
            P(None, TP),
            P(TP, None),
            P(),
            P(None, SEQ, None),
        ),
        out_specs=(
            P(None, SEQ, None),
            P(None, SEQ, None),
            P(),
            P(None, None, TP),
            P(None, TP),
            P(TP, None),
            P(),
            P(None, TP),
            P(None, TP),
            P(TP, None),
        ),
        check_vma=False,
    )
```

```python
import jax
import jax.numpy as jnp
from jax import lax
from jax.experimental import pallas as pl
from jax.experimental.pallas import tpu as pltpu
from jax.sharding import Mesh
from jax.sharding import PartitionSpec as P

epsilon = 1e-05
SEQ = ("z", "core")
TP = ("y", "x")
ALL = SEQ + TP
RING = 4
TPS = RING * RING
f32 = jnp.float32
bf16 = jnp.bfloat16


def turn(value, axis, steps):
    return lax.ppermute(value, axis, [(i, (i + steps) % RING) for i in range(RING)])


def ring_near(value, axis):
    return turn(value, axis, 3), turn(value, axis, 1)


def ring_far(near, axes):
    half = near[0].shape[0] // 2
    halves = assemble(
        near, (((1, 0, half),), ((0, half, half),), ((3, 0, half),), ((2, half, half),))
    )
    return tuple(turn(halves[i], axes[i // 2], (1, 3)[i % 2]) for i in range(4))


tied = lax.optimization_barrier


def plane_gather(value, early=(), launch=None, beside=()):
    half = value.shape[0] // 2
    top, bottom = assemble((value,), (((0, 0, half),), ((0, half, half),)))
    near = tuple(turn(top, "x", k) for k in (3, 2, 1)) + tuple(turn(bottom, "y", k) for k in (3, 2, 1))
    near, early = tied((near, early))
    launched, beside_last = launch(early) if launch else ((), ())
    top, bottom = assemble(
        (top, bottom) + near,
        (
            ((0, 0, half), (2, 0, half), (3, 0, half), (4, 0, half)),
            ((1, 0, half), (5, 0, half), (6, 0, half), (7, 0, half)),
        ),
    )
    near = ring_near(top, "y") + ring_near(bottom, "x")
    near, launched, beside = tied((near, launched, beside))
    far = ring_far(near, ("y", "x"))
    far, beside_last = tied((far, beside_last))
    return [top, near[0], near[1], bottom, near[2], near[3]], list(far), launched, beside_last, beside


def assemble(sources, plans):
    width, kind = sources[0].shape[1], sources[0].dtype
    copies = sum(len(plan) for plan in plans)

    def body(*refs):
        refs, sems = refs[:-1], refs[-1]
        started = []
        for out, plan in zip(refs[len(sources) :], plans):
            at = 0
            for source, start, rows in plan:
                copy = pltpu.make_async_copy(
                    refs[source].at[pl.ds(start, rows)],
                    out.at[pl.ds(at, rows)],
                    sems.at[len(started)],
                )
                copy.start()
                started.append(copy)
                at += rows
        for copy in started:
            copy.wait()

    shapes = [
        jax.ShapeDtypeStruct((sum(rows for _, _, rows in plan), width), kind) for plan in plans
    ]
    return pl.pallas_call(
        body,
        in_specs=[pl.BlockSpec(memory_space=pl.ANY)] * len(sources),
        out_specs=[pl.BlockSpec(memory_space=pl.ANY)] * len(plans),
        out_shape=shapes,
        scratch_shapes=[pltpu.SemaphoreType.DMA((copies,))],
        compiler_params=pltpu.CompilerParams(vmem_limit_bytes=2 * 1024 * 1024),
        cost_estimate=pl.CostEstimate(
            flops=0, bytes_accessed=4 * sum(x.size for x in shapes), transcendentals=0
        ),
        name="assemble",
    )(*sources)


def add_halves(blocks, moved):
    half, width = moved[0].shape
    count = len(blocks)

    def body(*refs):
        ins, more, outs = refs[:count], refs[count : 2 * count], refs[2 * count : 3 * count]
        held, added, in_sems, more_sems, out_sems = refs[3 * count :]

        def rows(ref, i):
            return ref.at[pl.ds(half * (i % 2), half)]

        loads = []
        for i in range(count):
            one = pltpu.make_async_copy(rows(ins[i], i), held.at[i], in_sems.at[i])
            two = pltpu.make_async_copy(more[i], added.at[i], more_sems.at[i])
            one.start()
            two.start()
            loads.append((one, two))
        stores = []
        for i in range(count):
            for load in loads[i]:
                load.wait()
            held[i] = (held[i].astype(f32) + added[i].astype(f32)).astype(bf16)
            store = pltpu.make_async_copy(held.at[i], rows(outs[i], i), out_sems.at[i])
            store.start()
            stores.append(store)
        for store in stores:
            store.wait()

    return pl.pallas_call(
        body,
        in_specs=[pl.BlockSpec(memory_space=pl.ANY)] * (2 * count),
        out_specs=[pl.BlockSpec(memory_space=pl.ANY)] * count,
        out_shape=[jax.ShapeDtypeStruct(x.shape, x.dtype) for x in blocks],
        input_output_aliases={i: i for i in range(count)},
        scratch_shapes=[
            pltpu.VMEM((count, half, width), bf16),
            pltpu.VMEM((count, half, width), bf16),
            pltpu.SemaphoreType.DMA((count,)),
            pltpu.SemaphoreType.DMA((count,)),
            pltpu.SemaphoreType.DMA((count,)),
        ],
        compiler_params=pltpu.CompilerParams(vmem_limit_bytes=8 * 1024 * 1024),
        cost_estimate=pl.CostEstimate(
            flops=count * half * width, bytes_accessed=6 * count * half * width, transcendentals=0
        ),
        name="add_halves",
    )(*blocks, *moved)


def scatter_far(pieces, axes):
    return tied(
        tuple(turn(pieces[i], axes[i // 2], (1, 3)[i % 2]) for i in range(4))
    )


def scatter_near(blocks, moved, axes):
    blocks = add_halves(blocks, moved)
    return tuple(turn(blocks[i], axes[i // 2], (1, 3)[i % 2]) for i in range(4))


def in_vmem(count):
    return [pl.BlockSpec(memory_space=pltpu.VMEM)] * count


def whole(*shapes):
    return [
        pl.BlockSpec(
            shape, lambda *_, rank=len(shape): (0,) * rank, pipeline_mode=pl.Buffered(buffer_count=1)
        )
        for shape in shapes
    ]


def hbm_call(body, operands, outs, megabytes, flops, name):
    def outer(*refs):
        n, m = len(operands), len(outs)
        held, held_outs = refs[n + m : 2 * n + m], refs[2 * n + m : 2 * n + 2 * m]
        sems = refs[-1]
        loads = [pltpu.make_async_copy(refs[i], held[i], sems.at[i]) for i in range(n)]
        for load in loads:
            load.start()
        for load in loads:
            load.wait()
        body(*held, *held_outs)
        stores = [
            pltpu.make_async_copy(held_outs[i], refs[n + i], sems.at[n + i]) for i in range(m)
        ]
        for store in stores:
            store.start()
        for store in stores:
            store.wait()

    arrays = list(operands) + list(outs)
    return pl.pallas_call(
        outer,
        in_specs=[pl.BlockSpec(memory_space=pltpu.HBM)] * len(operands),
        out_specs=[pl.BlockSpec(memory_space=pltpu.HBM)] * len(outs),
        out_shape=list(outs),
        scratch_shapes=[pltpu.VMEM(x.shape, x.dtype) for x in arrays]
        + [pltpu.SemaphoreType.DMA((len(arrays),))],
        compiler_params=pltpu.CompilerParams(vmem_limit_bytes=megabytes * 1024 * 1024),
        cost_estimate=pl.CostEstimate(
            flops=flops,
            bytes_accessed=sum(x.size * x.dtype.itemsize for x in arrays),
            transcendentals=0,
        ),
        name=name,
    )(*operands)


def ring_sums(own, one, other):
    rows, width = own.shape
    step = rows // RING
    cuts = tuple(step * k for k in range(RING + 1))

    def body(own_ref, one_ref, other_ref, *outs):
        for out, low, high in zip(outs, cuts[:-1], cuts[1:]):
            total = own_ref[low:high, :].astype(f32) + (
                one_ref[low:high, :].astype(f32) + other_ref[low:high, :].astype(f32)
            )
            out[...] = total.astype(out.dtype)

    return pl.pallas_call(
        body,
        grid=(1,),
        in_specs=whole(*[own.shape] * 3),
        out_specs=whole(*((high - low, width) for low, high in zip(cuts[:-1], cuts[1:]))),
        out_shape=[
            jax.ShapeDtypeStruct((high - low, width), f32 if low == 0 else bf16)
            for low, high in zip(cuts[:-1], cuts[1:])
        ],
        compiler_params=pltpu.CompilerParams(vmem_limit_bytes=10 * 1024 * 1024),
        cost_estimate=pl.CostEstimate(
            flops=2 * rows * width, bytes_accessed=8 * rows * width, transcendentals=0
        ),
        name="ring_sums",
    )(own, one, other)


def swap_cores(value):
    return lax.ppermute(value, "core", [(0, 1), (1, 0)])


CHUNKS = ((0, 0), (0, 1), (0, 3), (1, 0), (1, 1), (1, 3), (0, 2), (1, 2))


def plane_starts(half):
    y, x = lax.axis_index("y"), lax.axis_index("x")
    side = jnp.array([s for s, _ in CHUNKS for _ in range(RING)], jnp.int32)
    outer = jnp.array([k for _, k in CHUNKS for _ in range(RING)], jnp.int32)
    inner = jnp.array([k for _ in CHUNKS for k in range(RING)], jnp.int32)
    row = (jnp.where(side == 0, outer, inner) + y) % RING
    column = (jnp.where(side == 0, inner, outer) + x) % RING
    return (2 * (row * RING + column) + side) * half


def relative_rows(rows, starts, weight, split):
    half, width = rows.shape[0] // TPS // 2, rows.shape[1]
    count, units = rows.shape[0], weight.shape[0]
    slots = 8

    def body(table, source, weight_ref, low_a, low_b, hidden_a, hidden_b, held, lows, hiddens, *sems):
        sems, low_sems, hidden_sems = sems
        def copy(i):
            start = pl.multiple_of(table[i], half)
            return pltpu.make_async_copy(
                source.at[pl.ds(start, half)], held.at[i % slots], sems.at[i % slots]
            )

        for i in range(slots):
            copy(i).start()
        outs = []
        for i in range(0, 2 * TPS, RING):
            parts = []
            for j in range(i, i + RING):
                copy(j).wait()
                parts.append(held[j % slots].astype(bf16))
            low = jnp.concatenate(parts, axis=0)
            for j in range(i + slots, min(i + slots + RING, 2 * TPS)):
                copy(j).start()
            at, k = i * half, i // RING
            to_low, to_hidden = (low_a, hidden_a) if at < split else (low_b, hidden_b)
            at = at if at < split else at - split
            lows[k] = low
            hiddens[k] = dot(low, weight_ref[...], 1, 1)
            rows = pl.ds(at, RING * half)
            out = pltpu.make_async_copy(lows.at[k], to_low.at[rows], low_sems.at[k])
            out.start()
            outs.append(out)
            out = pltpu.make_async_copy(hiddens.at[k], to_hidden.at[rows], hidden_sems.at[k])
            out.start()
            outs.append(out)
        for out in outs:
            out.wait()

    return pl.pallas_call(
        body,
        grid_spec=pltpu.PrefetchScalarGridSpec(
            num_scalar_prefetch=1,
            grid=(1,),
            in_specs=[
                pl.BlockSpec(memory_space=pltpu.HBM),
                pl.BlockSpec(memory_space=pltpu.VMEM),
            ],
            out_specs=[pl.BlockSpec(memory_space=pltpu.HBM)] * 4,
            scratch_shapes=[
                pltpu.VMEM((slots, half, width), f32),
                pltpu.VMEM((2 * TPS // RING, RING * half, width), bf16),
                pltpu.VMEM((2 * TPS // RING, RING * half, units), f32),
                pltpu.SemaphoreType.DMA((slots,)),
                pltpu.SemaphoreType.DMA((2 * TPS // RING,)),
                pltpu.SemaphoreType.DMA((2 * TPS // RING,)),
            ],
        ),
        out_shape=[
            jax.ShapeDtypeStruct((split, width), bf16),
            jax.ShapeDtypeStruct((count - split, width), bf16),
            jax.ShapeDtypeStruct((split, units), f32),
            jax.ShapeDtypeStruct((count - split, units), f32),
        ],
        compiler_params=pltpu.CompilerParams(vmem_limit_bytes=16 * 1024 * 1024),
        cost_estimate=pl.CostEstimate(
            flops=2 * rows.size * units, bytes_accessed=rows.size * 6, transcendentals=0
        ),
        name="relative_rows",
    )(starts, rows, weight)


def absolute_rows(chunks, starts):
    total, width = sum(chunk.shape[0] for chunk in chunks), chunks[0].shape[1]
    half = total // TPS // 2
    slots = 16
    pieces = [(k, j) for k, chunk in enumerate(chunks) for j in range(chunk.shape[0] // half)]

    def body(table, *refs):
        parts, out, held, sems = refs[: len(chunks)], refs[-3], refs[-2], refs[-1]

        def copy(i):
            start = pl.multiple_of(table[i], half)
            return pltpu.make_async_copy(
                held.at[i % slots], out.at[pl.ds(start, half)], sems.at[i % slots]
            )

        for i, (k, j) in enumerate(pieces):
            if i >= slots:
                copy(i - slots).wait()
            held[i % slots] = parts[k][j * half : (j + 1) * half, :].astype(f32)
            copy(i).start()
        for i in range(2 * TPS - slots, 2 * TPS):
            copy(i).wait()

    return pl.pallas_call(
        body,
        grid_spec=pltpu.PrefetchScalarGridSpec(
            num_scalar_prefetch=1,
            grid=(1,),
            in_specs=[pl.BlockSpec(memory_space=pltpu.VMEM)] * len(chunks),
            out_specs=pl.BlockSpec(memory_space=pl.ANY),
            scratch_shapes=[
                pltpu.VMEM((slots, half, width), f32),
                pltpu.SemaphoreType.DMA((slots,)),
            ],
        ),
        out_shape=jax.ShapeDtypeStruct((total, width), f32),
        compiler_params=pltpu.CompilerParams(vmem_limit_bytes=7 * 1024 * 1024),
        cost_estimate=pl.CostEstimate(
            flops=total * width, bytes_accessed=total * width * 6, transcendentals=0
        ),
        name="absolute_rows",
    )(starts, *chunks)


def norm_and_project(rows, gain, weight):
    count, width = rows.shape
    chans = weight.shape[0]
    step = 256

    def body(rows_ref, gain_ref, weight_ref, normed_ref, out_ref):
        block = rows_ref[...]
        inverse = lax.rsqrt(jnp.mean(block * block, axis=-1, keepdims=True) + epsilon)
        normed = (block * inverse * gain_ref[...]).astype(bf16)
        normed_ref[...] = normed
        out_ref[...] = dot(weight_ref[...], normed, 1, 1)

    return pl.pallas_call(
        body,
        grid=(count // step,),
        in_specs=[
            pl.BlockSpec((step, width), lambda i: (i, 0)),
            pl.BlockSpec((1, width), lambda i: (0, 0)),
            pl.BlockSpec((chans, width), lambda i: (0, 0)),
        ],
        out_specs=[
            pl.BlockSpec((step, width), lambda i: (i, 0)),
            pl.BlockSpec((chans, step), lambda i: (0, i)),
        ],
        out_shape=[
            jax.ShapeDtypeStruct((count, width), bf16),
            jax.ShapeDtypeStruct((chans, count), f32),
        ],
        compiler_params=pltpu.CompilerParams(vmem_limit_bytes=6 * 1024 * 1024),
        cost_estimate=pl.CostEstimate(
            flops=2 * count * width * chans, bytes_accessed=6 * count * width, transcendentals=0
        ),
        name="norm_and_project",
    )(rows, gain.reshape(1, width), weight)


def mixer_gates(rows, weight, taps, mask_one, mask_two):
    own, width = mask_one.shape[0], rows.shape[1]
    chans = taps.shape[1]

    def body(rows_ref, weight_ref, taps_ref, one_ref, two_ref, gates_ref, lags_ref, conv_ref):
        b_gate = dot(rows_ref[...], weight_ref[:chans, :], 1, 1)
        c_gate = dot(rows_ref[8:, :], weight_ref[chans : 2 * chans, :], 1, 1)
        x_gate = dot(rows_ref[...], weight_ref[2 * chans :, :], 1, 1)
        product = (b_gate * x_gate).astype(bf16).astype(f32)
        one = one_ref[...] * product[7 : 7 + own]
        two = two_ref[...] * product[6 : 6 + own]
        product = product[8:]
        gates_ref[0] = b_gate[8:]
        gates_ref[1] = c_gate
        gates_ref[2] = x_gate[8:]
        lags_ref[0] = product
        lags_ref[1] = one
        lags_ref[2] = two
        conv_ref[...] = taps_ref[0:1, :] * product + taps_ref[1:2, :] * one + taps_ref[2:3, :] * two

    operands = (rows, weight, taps, mask_one, mask_two)
    outs = [
        jax.ShapeDtypeStruct((3, own, chans), f32),
        jax.ShapeDtypeStruct((3, own, chans), f32),
        jax.ShapeDtypeStruct((own, chans), f32),
    ]
    return pl.pallas_call(
        body,
        grid=(1,),
        in_specs=whole(*(x.shape for x in operands)),
        out_specs=whole(*(x.shape for x in outs)),
        out_shape=outs,
        compiler_params=pltpu.CompilerParams(vmem_limit_bytes=28 * 1024 * 1024),
        cost_estimate=pl.CostEstimate(
            flops=6 * own * width * chans, bytes_accessed=6 * width * chans, transcendentals=0
        ),
        name="mixer_gates",
    )(*operands)


def residual_back(own_sums, moved, residual, inverse, gain, grad, weight, c_rows, mask_one, mask_two):
    own, width = residual.shape
    half = own // 2
    chans = weight.shape[0]

    def body(*refs):
        sums, moved_refs, refs = refs[:2], refs[2:8], refs[8:]
        res_ref, inv_ref, gain_ref, grad_ref, weight_ref, gates_ref, one_ref, two_ref = refs[:8]
        block_ref, d_res_ref, low_ref, part_ref, mixer_ref, edge_ref = refs[8:]
        parts = []
        for i in range(2):
            rows = slice(i * half, (i + 1) * half)
            total = sums[i][...]
            for part in moved_refs[3 * i : 3 * i + 3]:
                total = total + part[...].astype(f32)
            d_norm, ffn = total[:, :width], total[:, width:]
            res, inv = res_ref[rows, :], inv_ref[rows, :]
            block_ref[rows, :] = (res + ffn).astype(bf16)
            parts.append(jnp.sum(d_norm * res * inv, axis=0, keepdims=True))
            scaled = gain_ref[...] * d_norm
            mean = jnp.mean(scaled * res, axis=-1, keepdims=True)
            d_res = grad_ref[rows, :] + inv * (scaled - res * inv * inv * mean)
            d_res_ref[rows, :] = d_res
            low_ref[rows, :] = d_res.astype(bf16)
        part_ref[...] = parts[0] + parts[1]
        d_mixer = dot(low_ref[...], weight_ref[...], 1, 1)
        mixer_ref[...] = d_mixer
        d_conv = d_mixer[:8] * gates_ref[...]
        edge_ref[0:8, :] = one_ref[:8, :] * d_conv
        edge_ref[8:16, :] = two_ref[:8, :] * d_conv

    operands = (*own_sums, *moved, residual, inverse, gain, grad, weight, c_rows, mask_one, mask_two)
    outs = [
        jax.ShapeDtypeStruct((own, width), bf16),
        jax.ShapeDtypeStruct((own, width), f32),
        jax.ShapeDtypeStruct((own, width), bf16),
        jax.ShapeDtypeStruct((1, width), f32),
        jax.ShapeDtypeStruct((own, chans), f32),
        jax.ShapeDtypeStruct((16, chans), f32),
    ]
    return hbm_call(body, operands, outs, 60, 2 * own * width * chans, "residual_back")


def mixer_back(
    d_mixer, edges, gates, lags, conv, mask_one, mask_two, taps, weight, rows, gain, d_res, second, halves
):
    own, width = rows.shape
    chans = d_mixer.shape[1]
    per = chans // TPS
    extra = 2 * width // own + 8

    def body(*refs):
        mixer_ref, edge_ref, gates_ref, lags_ref, conv_ref, one_ref, two_ref = refs[:7]
        taps_ref, weight_ref, rows_ref, gain_ref, d_res_ref, second_ref, halves_ref = refs[7:14]
        out_ref, send_ref, grads_ref = refs[14:]
        d_mix = mixer_ref[...]
        d_conv = d_mix * gates_ref[1]
        lag_one = one_ref[...] * d_conv
        lag_two = two_ref[...] * d_conv
        ahead_one = jnp.concatenate([lag_one[1:], edge_ref[0:1, :]], axis=0)
        ahead_two = jnp.concatenate([lag_two[2:], edge_ref[8:10, :]], axis=0)
        d_product = (
            taps_ref[0:1, :] * d_conv + taps_ref[1:2, :] * ahead_one + taps_ref[2:3, :] * ahead_two
        )
        grads_ref[0] = (d_product * gates_ref[2]).astype(bf16)
        grads_ref[1] = (d_mix * conv_ref[...]).astype(bf16)
        grads_ref[2] = (d_product * gates_ref[0]).astype(bf16)
        d_norm = dot(grads_ref[0], weight_ref[:chans, :], 1, 0)
        d_norm = d_norm + dot(grads_ref[1], weight_ref[chans : 2 * chans, :], 1, 0)
        d_norm = d_norm + dot(grads_ref[2], weight_ref[2 * chans :, :], 1, 0)
        block = rows_ref[...]
        inverse = lax.rsqrt(jnp.mean(block * block, axis=-1, keepdims=True) + epsilon)
        first = jnp.sum(d_norm * block * inverse, axis=0, keepdims=True)
        scaled = gain_ref[...] * d_norm
        mean = jnp.mean(scaled * block, axis=-1, keepdims=True)
        out = d_res_ref[...] + inverse * (scaled - block * inverse * inverse * mean)
        out_ref[...] = out.astype(bf16)
        tap_sums = [jnp.sum(d_conv * lags_ref[k], axis=0, keepdims=True) for k in range(3)]
        sums = jnp.concatenate(tap_sums + [jnp.zeros((5, chans), f32)], axis=0)
        gains = []
        for value in (first, second_ref[...]):
            gains += [value[:, k * own : (k + 1) * own] for k in range(width // own)]
        gains = jnp.concatenate(gains, axis=0)
        for g in range(3):
            turned = grads_ref[g].astype(f32).T.astype(bf16)
            for j in range(TPS):
                send_ref[j, g * per : (g + 1) * per, :] = turned[j * per : (j + 1) * per]
        for j in range(TPS):
            pair = j // 2 * 2 * per
            tail = jnp.concatenate([gains, sums[:, pair : pair + 2 * per]], axis=0)
            send_ref[j, 3 * per : 3 * per + extra, :] = tail.astype(bf16)
            for k in range(width // own):
                at = 3 * per + extra + k * halves.shape[1]
                send_ref[j, at : at + halves.shape[1], :] = halves_ref[j, :, k * own : (k + 1) * own]

    operands = (d_mixer, edges, gates, lags, conv, mask_one, mask_two, taps, weight, rows, gain, d_res, second, halves)
    outs = [
        jax.ShapeDtypeStruct((own, width), bf16),
        jax.ShapeDtypeStruct((TPS, 3 * per + extra + halves.shape[1] * width // own, own), bf16),
    ]
    return pl.pallas_call(
        body,
        grid=(1,),
        in_specs=whole(*(x.shape for x in operands)),
        out_specs=whole(*(x.shape for x in outs)),
        out_shape=outs,
        scratch_shapes=[pltpu.VMEM((3, own, chans), bf16)],
        compiler_params=pltpu.CompilerParams(vmem_limit_bytes=36 * 1024 * 1024),
        cost_estimate=pl.CostEstimate(
            flops=6 * own * width * chans, bytes_accessed=6 * width * chans, transcendentals=0
        ),
        name="mixer_back",
    )(*operands)


def feed_forward(norms, d_hidden, gate_t, up_t, down, pieces):
    count, ff = d_hidden.shape
    width = down.shape[1]
    step = norms[0].shape[0]
    piece = count // pieces

    def body(*refs):
        norm_refs, rest = refs[: len(norms)], refs[len(norms) :]
        d_hbm, gate_ref, up_ref, down_ref = rest[:4]
        outs, (d_gate_ref, d_up_ref, hidden_ref, d_ref, sem) = rest[4:-5], rest[-5:]
        load = pltpu.make_async_copy(d_hbm, d_ref, sem)
        load.start()
        for k, norm_ref in enumerate(norm_refs):
            part = slice(k * step, (k + 1) * step)
            norm = norm_ref[...]
            gate = dot(norm, gate_ref[...], 1, 1)
            up = dot(norm, up_ref[...], 1, 1)
            if k == 0:
                load.wait()
            d_part = d_ref[part, :]
            sig = jax.nn.sigmoid(gate)
            act = gate * sig
            hidden = (act * up).astype(bf16)
            d_gate = (d_part * up * sig * (1.0 + gate * (1.0 - sig))).astype(bf16)
            d_up = (d_part * act).astype(bf16)
            d_gate_ref[part, :] = d_gate
            d_up_ref[part, :] = d_up
            hidden_ref[part, :] = hidden
            d_norm = (dot(d_gate, gate_ref[...], 1, 0) + dot(d_up, up_ref[...], 1, 0)).astype(bf16)
            ffn = dot(hidden, down_ref[...], 1, 0, bf16)
            first = k * step // piece
            for j in range(max(1, step // piece)):
                inside = slice(j * piece, (j + 1) * piece)
                outs[first + j][:, :width] = d_norm[inside]
                outs[first + j][:, width:] = ffn[inside]

    outs = pl.pallas_call(
        body,
        in_specs=in_vmem(len(norms)) + [pl.BlockSpec(memory_space=pltpu.HBM)] + in_vmem(3),
        out_specs=in_vmem(pieces + 3),
        out_shape=[jax.ShapeDtypeStruct((piece, 2 * width), bf16)] * pieces
        + [jax.ShapeDtypeStruct((count, ff), bf16)] * 3,
        scratch_shapes=[pltpu.VMEM(d_hidden.shape, f32), pltpu.SemaphoreType.DMA(())],
        compiler_params=pltpu.CompilerParams(vmem_limit_bytes=12 * 1024 * 1024),
        cost_estimate=pl.CostEstimate(
            flops=10 * count * width * ff,
            bytes_accessed=count * width * 6,
            transcendentals=count * ff,
        ),
        name="feed_forward",
    )(*norms, d_hidden, gate_t, up_t, down)
    return outs[:pieces], outs[pieces:]


def dot(left, right, left_dim, right_dim, kind=f32):
    out = lax.dot_general(
        left, right, (((left_dim,), (right_dim,)), ((), ())), preferred_element_type=f32
    )
    return out.astype(kind)


def doc_index(doc_starts, positions):
    hits = (doc_starts[:, None, :] <= positions[None, :, None]).astype(jnp.int32)
    return jnp.sum(hits, axis=-1) - 1


def shards(
    block_input,
    first_gain,
    in_weight,
    conv_taps,
    out_weight,
    second_gain,
    gate_weight,
    up_weight,
    down_weight,
    doc_starts,
    out_cotangent,
):
    seqs, seg, width = block_input.shape
    chans = in_weight.shape[2]
    ff = gate_weight.shape[1]
    count = seqs * seg
    own = count // TPS
    per_seq = TPS // seqs
    y, x = lax.axis_index("y"), lax.axis_index("x")
    place = y * RING + x
    seq = lax.axis_index(SEQ)
    starts = plane_starts(own // 2)

    positions = seq * seg + jnp.arange(seg, dtype=jnp.int32)
    current = doc_index(doc_starts, positions)
    one_back = (doc_index(doc_starts, positions - 1) == current).astype(f32)
    two_back = (doc_index(doc_starts, positions - 2) == current).astype(f32)

    channels = TPS * chans
    is_low = lax.axis_index("core") == 0
    out_half = lax.dynamic_slice_in_dim(
        out_weight, lax.axis_index("core") * (chans // 2), chans // 2, axis=0
    )
    out_mine = jnp.broadcast_to(out_half[None], (TPS, chans // 2, width))
    out_mine = lax.all_to_all(out_mine, TP, 0, 0, tiled=True)
    in_wt = jnp.transpose(in_weight, (1, 2, 0))
    share = chans // 8
    taps_high = lax.reduce_precision(conv_taps, 8, 7)
    taps_mid = lax.reduce_precision(conv_taps - taps_high, 8, 7)
    taps_low = lax.reduce_precision(conv_taps - taps_high - taps_mid, 8, 7)
    taps_row = jnp.stack([taps_high, taps_mid, taps_low], axis=0).astype(bf16).reshape(1, 9 * chans)
    taps_row = jnp.pad(taps_row, ((0, share - 1), (0, width - 9 * chans)))
    in_share = lax.dynamic_slice_in_dim(in_wt, seq * share, share, axis=1)
    in_share = jnp.concatenate([in_share, taps_row[None]], axis=0)
    in_all = lax.all_gather(in_share, ALL, axis=0, tiled=False)
    in_all = in_all.reshape(8, TPS, 4, share, width)
    taps = in_all[0, :, 3, 0, : 9 * chans].astype(f32).reshape(TPS, 3, 3, chans)
    taps = (taps[:, 0] + taps[:, 1]) + taps[:, 2]
    taps = taps.transpose(1, 0, 2).reshape(3, channels)
    in_all = in_all[:, :, :3].transpose(2, 1, 0, 3, 4).reshape(3 * channels, width)

    flat_input = block_input.reshape(count, width)
    in_flat = in_wt.reshape(3 * chans, width)
    normed1, projected = norm_and_project(flat_input, first_gain, in_flat)
    projected, out_mine = tied((projected, out_mine))
    out_theirs = swap_cores(out_mine)
    out_all = jnp.stack(
        [jnp.where(is_low, out_mine, out_theirs), jnp.where(is_low, out_theirs, out_mine)], axis=1
    ).reshape(channels, width)
    last = normed1.reshape(seqs, seg, width)[:, seg - 8 :]
    carried = lax.ppermute(
        last, ALL, [(i, i + TPS) for i in range(7 * TPS)]
    )
    mixer_blocks = []
    for s in range(seqs):
        proj = projected[:, s * seg : (s + 1) * seg]
        edge = dot(in_flat, carried[s], 1, 1)
        product = (proj[:chans] * proj[2 * chans :]).astype(bf16)
        before = (edge[:chans] * edge[2 * chans :]).astype(bf16)
        extended = jnp.concatenate([before[:, 6:], product], axis=1).astype(f32)
        convolved = (
            conv_taps[0][:, None] * product.astype(f32)
            + conv_taps[1][:, None] * one_back[s] * extended[:, 1 : seg + 1]
            + conv_taps[2][:, None] * two_back[s] * extended[:, :seg]
        )
        mixed = (proj[chans : 2 * chans] * convolved).astype(bf16)
        mixer_blocks.append(mixed.reshape(chans, per_seq, own).transpose(1, 0, 2))
    mixer_blocks = jnp.concatenate(mixer_blocks, axis=0)
    mixer = lax.all_to_all(mixer_blocks, TP, 0, 0, tiled=True)
    mixer = mixer.reshape(channels, own)

    rows_in = lax.dynamic_slice_in_dim(flat_input, place * own, own, axis=0)
    residual = rows_in + dot(mixer, out_all, 0, 0)
    inverse_two = lax.rsqrt(jnp.mean(residual * residual, axis=-1, keepdims=True) + epsilon)
    normed2 = (residual * inverse_two * second_gain).astype(bf16)

    later = (normed2[0, 0].astype(f32) * 0.0).astype(jnp.int32)
    split = count * 3 // 4
    *grad_low, hidden_first, hidden_last = relative_rows(
        out_cotangent.reshape(count, width), starts + later, down_weight, split
    )
    gate_t, up_t = gate_weight.T, up_weight.T
    norm_first, norm_last, _, _, (hidden_first, hidden_last) = plane_gather(
        normed2, beside=(hidden_first, hidden_last)
    )
    sums_first, kept_first = feed_forward(
        norm_first, hidden_first, gate_t, up_t, down_weight, 6
    )
    piece = norm_last[0].shape[0]
    norm_last = assemble(
        norm_last, (((0, 0, piece), (1, 0, piece)), ((2, 0, piece), (3, 0, piece)))
    )
    norm_last, sums_first = tied((norm_last, sums_first))
    sums_last, kept_last = feed_forward(norm_last, hidden_last, gate_t, up_t, down_weight, 4)
    moved = scatter_far(sums_last, ("y", "x"))
    moved, kept_first, kept_last, norm_first, norm_last = tied(
        (moved, kept_first, kept_last, norm_first, norm_last)
    )
    rows = norm_last[0].shape[0]
    norm_first, norm_last = assemble(
        tuple(norm_first) + tuple(norm_last),
        (tuple((i, 0, rows) for i in range(6)), ((6, 0, rows), (7, 0, rows))),
    )
    ffn_grads = []
    for k in range(3):
        right_first = norm_first if k < 2 else grad_low[0]
        right_last = norm_last if k < 2 else grad_low[1]
        part = dot(kept_first[k], right_first, 0, 0) + dot(kept_last[k], right_last, 0, 0)
        ffn_grads.append(part.astype(bf16))
    ffn_grads = jnp.concatenate(ffn_grads + [jnp.zeros((32, width), bf16)], axis=0)
    ffn_grads = lax.psum_scatter(ffn_grads, SEQ, scatter_dimension=0, tiled=True)

    rows_n1 = lax.dynamic_slice_in_dim(normed1, place * own, own, axis=0)
    local_edge = lax.dynamic_slice_in_dim(normed1, place * own - 8, 8, axis=0)
    at_start = place % per_seq == 0
    edge_n1 = jnp.where(at_start, carried[place // per_seq], local_edge)
    rows_one = lax.dynamic_slice_in_dim(one_back.reshape(count, 1), place * own, own, axis=0)
    rows_two = lax.dynamic_slice_in_dim(two_back.reshape(count, 1), place * own, own, axis=0)
    rows_n1 = jnp.concatenate([edge_n1, rows_n1], axis=0)

    moved = scatter_near([sums_first[i] for i in (1, 2, 4, 5)], moved, ("y", "x"))
    gates, lags, conv = mixer_gates(rows_n1, in_all, taps, rows_one, rows_two)
    moved, gates, lags, conv = tied((moved, gates, lags, conv))
    top = ring_sums(sums_first[0], *moved[:2])
    bottom = ring_sums(sums_first[3], *moved[2:])
    moved = tuple(turn(top[k], "x", k) for k in (1, 2, 3))
    moved = moved + tuple(turn(bottom[k], "y", k) for k in (1, 2, 3))
    moved, ffn_grads = tied((moved, ffn_grads))

    grad_rows = lax.dynamic_slice_in_dim(
        out_cotangent.reshape(count, width), place * own, own, axis=0
    )
    block_rows, d_residual, d_low, second_part, d_mixer, edges = residual_back(
        (top[0], bottom[0]),
        moved,
        residual,
        inverse_two,
        second_gain.reshape(1, width),
        grad_rows,
        out_all,
        gates[1, :8],
        rows_one,
        rows_two,
    )
    block_output = lax.all_gather(block_rows, TP, axis=0, tiled=True)
    pairs = []
    for sq in range(8):
        for j in range(TPS):
            if j % per_seq:
                pairs.append((sq * TPS + j, sq * TPS + j - 1))
            elif sq:
                pairs.append((sq * TPS + j, (sq - 1) * TPS + j + per_seq - 1))
    edges = lax.ppermute(edges, ALL, pairs)
    out_part = dot(mixer, d_low, 1, 0, bf16).reshape(TPS, 2, chans // 2, width)
    theirs = swap_cores(jnp.where(is_low, out_part[:, 1], out_part[:, 0]))
    out_part = jnp.where(is_low, out_part[:, 0], out_part[:, 1]).astype(f32) + theirs.astype(f32)
    input_rows, exchanged = mixer_back(
        d_mixer,
        edges,
        gates,
        lags,
        conv,
        rows_one,
        rows_two,
        taps,
        in_all,
        rows_in,
        first_gain.reshape(1, width),
        d_residual,
        second_part,
        out_part.astype(bf16),
    )
    middle = 3 * chans // 2

    def exchange(early):
        exchanged, ffn_grads = early
        exchanged = lax.all_to_all(exchanged, TP, 0, 0, tiled=True)
        return exchanged, lax.all_gather(ffn_grads, SEQ, axis=0, tiled=True)

    input_first, input_last, exchanged, ffn_grads, block_output = plane_gather(
        input_rows, (exchanged, ffn_grads), exchange, block_output
    )
    received = exchanged[:, : 3 * chans].transpose(1, 0, 2)
    in_part = dot(received.reshape(3 * chans, count), normed1, 1, 0, bf16)
    small = jnp.sum(exchanged[:, 3 * chans :].astype(f32), axis=0).astype(bf16)
    out_part = small[24:].reshape(width // own, chans // 2, own).transpose(1, 0, 2)
    out_part = out_part.reshape(chans // 2, width)
    small = jnp.pad(small[:24].reshape(3, width), ((0, 5), (0, 0)))
    theirs = swap_cores(
        jnp.concatenate([jnp.where(is_low, in_part[middle:], in_part[:middle]), small], axis=0)
    )
    mine = jnp.where(is_low, in_part[:middle], in_part[middle:])
    mine = jnp.concatenate([mine, small], axis=0).astype(f32) + theirs.astype(f32)
    mine = jnp.concatenate([mine.astype(bf16), out_part], axis=0)
    by_z = jnp.broadcast_to(mine[None], (RING,) + mine.shape)
    by_z = lax.all_to_all(by_z, "z", 0, 0, tiled=True)
    block_output = block_output.astype(f32)
    gate_grad = ffn_grads[:ff].astype(f32).T
    up_grad = ffn_grads[ff : 2 * ff].astype(f32).T
    down_grad = ffn_grads[2 * ff : 3 * ff].astype(f32)
    input_grad = absolute_rows(input_first + input_last, starts)

    by_z = by_z.astype(f32)
    total = (by_z[0] + by_z[2]) + (by_z[1] + by_z[3])
    small = total[middle : middle + 8]
    mine = jnp.concatenate([total[:middle], total[middle + 8 :]], axis=0).astype(bf16)
    theirs = swap_cores(mine)
    low, high = jnp.where(is_low, mine, theirs), jnp.where(is_low, theirs, mine)
    low, high = low.astype(f32), high.astype(f32)
    in_grad = jnp.concatenate([low[:middle], high[:middle]], axis=0)
    in_grad = in_grad.reshape(3, chans, width).transpose(2, 0, 1)
    out_grad = jnp.concatenate([low[middle:], high[middle:]], axis=0)
    first_grad, second_grad = small[0], small[1]
    taps_grad = small[2].reshape(8, own)[:3]
    taps_grad = lax.dynamic_slice_in_dim(taps_grad, place % 2 * chans, chans, axis=1)

    return (
        block_output.reshape(seqs, seg, width),
        input_grad.reshape(seqs, seg, width),
        first_grad,
        in_grad,
        taps_grad,
        out_grad,
        second_grad,
        gate_grad,
        up_grad,
        down_grad,
    )


def solution(mesh):
    grid = Mesh(mesh.devices.reshape(4, 2, RING, RING), ALL)
    return jax.shard_map(
        shards,
        mesh=grid,
        in_specs=(
            P(None, SEQ, None),
            P(),
            P(None, None, TP),
            P(None, TP),
            P(TP, None),
            P(),
            P(None, TP),
            P(None, TP),
            P(TP, None),
            P(),
            P(None, SEQ, None),
        ),
        out_specs=(
            P(None, SEQ, None),
            P(None, SEQ, None),
            P(),
            P(None, None, TP),
            P(None, TP),
            P(TP, None),
            P(),
            P(None, TP),
            P(None, TP),
            P(TP, None),
        ),
        check_vma=False,
    )
```

```python
import jax
import jax.numpy as jnp
from jax import lax
from jax.experimental import pallas as pl
from jax.experimental.pallas import tpu as pltpu
from jax.sharding import Mesh
from jax.sharding import PartitionSpec as P

epsilon = 1e-05
SEQ = ("z", "core")
TP = ("y", "x")
ALL = SEQ + TP
RING = 4
TPS = RING * RING
f32 = jnp.float32
bf16 = jnp.bfloat16


def turn(value, axis, steps):
    return lax.ppermute(value, axis, [(i, (i + steps) % RING) for i in range(RING)])


def ring_near(value, axis):
    return turn(value, axis, 3), turn(value, axis, 1)


def ring_far(near, axes):
    half = near[0].shape[0] // 2
    halves = assemble(
        near, (((1, 0, half),), ((0, half, half),), ((3, 0, half),), ((2, half, half),))
    )
    return tuple(turn(halves[i], axes[i // 2], (1, 3)[i % 2]) for i in range(4))


tied = lax.optimization_barrier


def plane_gather(value, early=(), launch=None, beside=(), own=None):
    half = value.shape[0] // 2
    top, bottom = assemble((value,), (((0, 0, half),), ((0, half, half),)))
    near = tuple(turn(top, "x", k) for k in (3, 2, 1)) + tuple(turn(bottom, "y", k) for k in (3, 2, 1))
    near, early = tied((near, early))
    launched, beside_last = launch(early) if launch else ((), ())
    top, bottom = assemble(
        (top, bottom) + near,
        (
            ((0, 0, half), (2, 0, half), (3, 0, half), (4, 0, half)),
            ((1, 0, half), (5, 0, half), (6, 0, half), (7, 0, half)),
        ),
    )
    near = ring_near(top, "y") + ring_near(bottom, "x")
    if own:
        beside = (beside, own([top, bottom]))
    near, launched, beside = tied((near, launched, beside))
    far = ring_far(near, ("y", "x"))
    far, beside_last = tied((far, beside_last))
    return [top, bottom, *near], list(far), launched, beside_last, beside


def assemble(sources, plans):
    width, kind = sources[0].shape[1], sources[0].dtype
    copies = sum(len(plan) for plan in plans)

    def body(*refs):
        refs, sems = refs[:-1], refs[-1]
        started = []
        for out, plan in zip(refs[len(sources) :], plans):
            at = 0
            for source, start, rows in plan:
                copy = pltpu.make_async_copy(
                    refs[source].at[pl.ds(start, rows)],
                    out.at[pl.ds(at, rows)],
                    sems.at[len(started)],
                )
                copy.start()
                started.append(copy)
                at += rows
        for copy in started:
            copy.wait()

    shapes = [
        jax.ShapeDtypeStruct((sum(rows for _, _, rows in plan), width), kind) for plan in plans
    ]
    return pl.pallas_call(
        body,
        in_specs=[pl.BlockSpec(memory_space=pl.ANY)] * len(sources),
        out_specs=[pl.BlockSpec(memory_space=pl.ANY)] * len(plans),
        out_shape=shapes,
        scratch_shapes=[pltpu.SemaphoreType.DMA((copies,))],
        compiler_params=pltpu.CompilerParams(vmem_limit_bytes=2 * 1024 * 1024),
        cost_estimate=pl.CostEstimate(
            flops=0, bytes_accessed=4 * sum(x.size for x in shapes), transcendentals=0
        ),
        name="assemble",
    )(*sources)


def add_halves(blocks, moved):
    half, width = moved[0].shape
    count = len(blocks)

    def body(*refs):
        ins, more, outs = refs[:count], refs[count : 2 * count], refs[2 * count : 3 * count]
        held, added, in_sems, more_sems, out_sems = refs[3 * count :]

        def rows(ref, i):
            return ref.at[pl.ds(half * (i % 2), half)]

        loads = []
        for i in range(count):
            one = pltpu.make_async_copy(rows(ins[i], i), held.at[i], in_sems.at[i])
            two = pltpu.make_async_copy(more[i], added.at[i], more_sems.at[i])
            one.start()
            two.start()
            loads.append((one, two))
        stores = []
        for i in range(count):
            for load in loads[i]:
                load.wait()
            held[i] = (held[i].astype(f32) + added[i].astype(f32)).astype(bf16)
            store = pltpu.make_async_copy(held.at[i], rows(outs[i], i), out_sems.at[i])
            store.start()
            stores.append(store)
        for store in stores:
            store.wait()

    return pl.pallas_call(
        body,
        in_specs=[pl.BlockSpec(memory_space=pl.ANY)] * (2 * count),
        out_specs=[pl.BlockSpec(memory_space=pl.ANY)] * count,
        out_shape=[jax.ShapeDtypeStruct(x.shape, x.dtype) for x in blocks],
        input_output_aliases={i: i for i in range(count)},
        scratch_shapes=[
            pltpu.VMEM((count, half, width), bf16),
            pltpu.VMEM((count, half, width), bf16),
            pltpu.SemaphoreType.DMA((count,)),
            pltpu.SemaphoreType.DMA((count,)),
            pltpu.SemaphoreType.DMA((count,)),
        ],
        compiler_params=pltpu.CompilerParams(vmem_limit_bytes=8 * 1024 * 1024),
        cost_estimate=pl.CostEstimate(
            flops=count * half * width, bytes_accessed=6 * count * half * width, transcendentals=0
        ),
        name="add_halves",
    )(*blocks, *moved)


def scatter_far(pieces, axes):
    return tied(
        tuple(turn(pieces[i], axes[i // 2], (1, 3)[i % 2]) for i in range(4))
    )


def scatter_near(blocks, moved, axes):
    blocks = add_halves(blocks, moved)
    return tuple(turn(blocks[i], axes[i // 2], (1, 3)[i % 2]) for i in range(4))


def in_vmem(count):
    return [pl.BlockSpec(memory_space=pltpu.VMEM)] * count


def whole(*shapes):
    return [
        pl.BlockSpec(
            shape, lambda *_, rank=len(shape): (0,) * rank, pipeline_mode=pl.Buffered(buffer_count=1)
        )
        for shape in shapes
    ]


def hbm_call(body, operands, outs, megabytes, flops, name):
    def outer(*refs):
        n, m = len(operands), len(outs)
        held, held_outs = refs[n + m : 2 * n + m], refs[2 * n + m : 2 * n + 2 * m]
        sems = refs[-1]
        loads = [pltpu.make_async_copy(refs[i], held[i], sems.at[i]) for i in range(n)]
        for load in loads:
            load.start()
        for load in loads:
            load.wait()
        body(*held, *held_outs)
        stores = [
            pltpu.make_async_copy(held_outs[i], refs[n + i], sems.at[n + i]) for i in range(m)
        ]
        for store in stores:
            store.start()
        for store in stores:
            store.wait()

    arrays = list(operands) + list(outs)
    return pl.pallas_call(
        outer,
        in_specs=[pl.BlockSpec(memory_space=pltpu.HBM)] * len(operands),
        out_specs=[pl.BlockSpec(memory_space=pltpu.HBM)] * len(outs),
        out_shape=list(outs),
        scratch_shapes=[pltpu.VMEM(x.shape, x.dtype) for x in arrays]
        + [pltpu.SemaphoreType.DMA((len(arrays),))],
        compiler_params=pltpu.CompilerParams(vmem_limit_bytes=megabytes * 1024 * 1024),
        cost_estimate=pl.CostEstimate(
            flops=flops,
            bytes_accessed=sum(x.size * x.dtype.itemsize for x in arrays),
            transcendentals=0,
        ),
        name=name,
    )(*operands)


def ring_sums(own, one, other):
    rows, width = own.shape
    step = rows // RING
    cuts = tuple(step * k for k in range(RING + 1))

    def body(own_ref, one_ref, other_ref, *outs):
        for out, low, high in zip(outs, cuts[:-1], cuts[1:]):
            total = own_ref[low:high, :].astype(f32) + (
                one_ref[low:high, :].astype(f32) + other_ref[low:high, :].astype(f32)
            )
            out[...] = total.astype(out.dtype)

    return pl.pallas_call(
        body,
        grid=(1,),
        in_specs=whole(*[own.shape] * 3),
        out_specs=whole(*((high - low, width) for low, high in zip(cuts[:-1], cuts[1:]))),
        out_shape=[
            jax.ShapeDtypeStruct((high - low, width), f32 if low == 0 else bf16)
            for low, high in zip(cuts[:-1], cuts[1:])
        ],
        compiler_params=pltpu.CompilerParams(vmem_limit_bytes=10 * 1024 * 1024),
        cost_estimate=pl.CostEstimate(
            flops=2 * rows * width, bytes_accessed=8 * rows * width, transcendentals=0
        ),
        name="ring_sums",
    )(own, one, other)


def swap_cores(value):
    return lax.ppermute(value, "core", [(0, 1), (1, 0)])


CHUNKS = ((0, 0), (1, 0), (0, 1), (0, 3), (1, 1), (1, 3), (0, 2), (1, 2))


def plane_starts(half):
    y, x = lax.axis_index("y"), lax.axis_index("x")
    side = jnp.array([s for s, _ in CHUNKS for _ in range(RING)], jnp.int32)
    outer = jnp.array([k for _, k in CHUNKS for _ in range(RING)], jnp.int32)
    inner = jnp.array([k for _ in CHUNKS for k in range(RING)], jnp.int32)
    row = (jnp.where(side == 0, outer, inner) + y) % RING
    column = (jnp.where(side == 0, inner, outer) + x) % RING
    return (2 * (row * RING + column) + side) * half


def relative_rows(rows, starts, weight, split):
    half, width = rows.shape[0] // TPS // 2, rows.shape[1]
    count, units = rows.shape[0], weight.shape[0]
    slots = 8

    def body(table, source, weight_ref, low_a, low_b, hidden_a, hidden_b, held, lows, hiddens, *sems):
        sems, low_sems, hidden_sems = sems
        def copy(i):
            start = pl.multiple_of(table[i], half)
            return pltpu.make_async_copy(
                source.at[pl.ds(start, half)], held.at[i % slots], sems.at[i % slots]
            )

        for i in range(slots):
            copy(i).start()
        outs = []
        for i in range(0, 2 * TPS, RING):
            parts = []
            for j in range(i, i + RING):
                copy(j).wait()
                parts.append(held[j % slots].astype(bf16))
            low = jnp.concatenate(parts, axis=0)
            for j in range(i + slots, min(i + slots + RING, 2 * TPS)):
                copy(j).start()
            at, k = i * half, i // RING
            to_low, to_hidden = (low_a, hidden_a) if at < split else (low_b, hidden_b)
            at = at if at < split else at - split
            lows[k] = low
            hiddens[k] = dot(low, weight_ref[...], 1, 1)
            rows = pl.ds(at, RING * half)
            out = pltpu.make_async_copy(lows.at[k], to_low.at[rows], low_sems.at[k])
            out.start()
            outs.append(out)
            out = pltpu.make_async_copy(hiddens.at[k], to_hidden.at[rows], hidden_sems.at[k])
            out.start()
            outs.append(out)
        for out in outs:
            out.wait()

    return pl.pallas_call(
        body,
        grid_spec=pltpu.PrefetchScalarGridSpec(
            num_scalar_prefetch=1,
            grid=(1,),
            in_specs=[
                pl.BlockSpec(memory_space=pltpu.HBM),
                pl.BlockSpec(memory_space=pltpu.VMEM),
            ],
            out_specs=[pl.BlockSpec(memory_space=pltpu.HBM)] * 4,
            scratch_shapes=[
                pltpu.VMEM((slots, half, width), f32),
                pltpu.VMEM((2 * TPS // RING, RING * half, width), bf16),
                pltpu.VMEM((2 * TPS // RING, RING * half, units), f32),
                pltpu.SemaphoreType.DMA((slots,)),
                pltpu.SemaphoreType.DMA((2 * TPS // RING,)),
                pltpu.SemaphoreType.DMA((2 * TPS // RING,)),
            ],
        ),
        out_shape=[
            jax.ShapeDtypeStruct((split, width), bf16),
            jax.ShapeDtypeStruct((count - split, width), bf16),
            jax.ShapeDtypeStruct((split, units), f32),
            jax.ShapeDtypeStruct((count - split, units), f32),
        ],
        compiler_params=pltpu.CompilerParams(vmem_limit_bytes=16 * 1024 * 1024),
        cost_estimate=pl.CostEstimate(
            flops=2 * rows.size * units, bytes_accessed=rows.size * 6, transcendentals=0
        ),
        name="relative_rows",
    )(starts, rows, weight)


def absolute_rows(chunks, starts):
    total, width = sum(chunk.shape[0] for chunk in chunks), chunks[0].shape[1]
    half = total // TPS // 2
    slots = 16
    pieces = [(k, j) for k, chunk in enumerate(chunks) for j in range(chunk.shape[0] // half)]

    def body(table, *refs):
        parts, out, held, sems = refs[: len(chunks)], refs[-3], refs[-2], refs[-1]

        def copy(i):
            start = pl.multiple_of(table[i], half)
            return pltpu.make_async_copy(
                held.at[i % slots], out.at[pl.ds(start, half)], sems.at[i % slots]
            )

        for i, (k, j) in enumerate(pieces):
            if i >= slots:
                copy(i - slots).wait()
            held[i % slots] = parts[k][j * half : (j + 1) * half, :].astype(f32)
            copy(i).start()
        for i in range(2 * TPS - slots, 2 * TPS):
            copy(i).wait()

    return pl.pallas_call(
        body,
        grid_spec=pltpu.PrefetchScalarGridSpec(
            num_scalar_prefetch=1,
            grid=(1,),
            in_specs=[pl.BlockSpec(memory_space=pltpu.VMEM)] * len(chunks),
            out_specs=pl.BlockSpec(memory_space=pl.ANY),
            scratch_shapes=[
                pltpu.VMEM((slots, half, width), f32),
                pltpu.SemaphoreType.DMA((slots,)),
            ],
        ),
        out_shape=jax.ShapeDtypeStruct((total, width), f32),
        compiler_params=pltpu.CompilerParams(vmem_limit_bytes=7 * 1024 * 1024),
        cost_estimate=pl.CostEstimate(
            flops=total * width, bytes_accessed=total * width * 6, transcendentals=0
        ),
        name="absolute_rows",
    )(starts, *chunks)


def norm_and_project(rows, gain, weight):
    count, width = rows.shape
    chans = weight.shape[0]
    step = 256

    def body(rows_ref, gain_ref, weight_ref, normed_ref, out_ref):
        block = rows_ref[...]
        inverse = lax.rsqrt(jnp.mean(block * block, axis=-1, keepdims=True) + epsilon)
        normed = (block * inverse * gain_ref[...]).astype(bf16)
        normed_ref[...] = normed
        out_ref[...] = dot(weight_ref[...], normed, 1, 1)

    return pl.pallas_call(
        body,
        grid=(count // step,),
        in_specs=[
            pl.BlockSpec((step, width), lambda i: (i, 0)),
            pl.BlockSpec((1, width), lambda i: (0, 0)),
            pl.BlockSpec((chans, width), lambda i: (0, 0)),
        ],
        out_specs=[
            pl.BlockSpec((step, width), lambda i: (i, 0)),
            pl.BlockSpec((chans, step), lambda i: (0, i)),
        ],
        out_shape=[
            jax.ShapeDtypeStruct((count, width), bf16),
            jax.ShapeDtypeStruct((chans, count), f32),
        ],
        compiler_params=pltpu.CompilerParams(vmem_limit_bytes=6 * 1024 * 1024),
        cost_estimate=pl.CostEstimate(
            flops=2 * count * width * chans, bytes_accessed=6 * count * width, transcendentals=0
        ),
        name="norm_and_project",
    )(rows, gain.reshape(1, width), weight)


def mixer_gates(rows, weight, taps, mask_one, mask_two):
    own, width = mask_one.shape[0], rows.shape[1]
    chans = taps.shape[1]

    def body(rows_ref, weight_ref, taps_ref, one_ref, two_ref, gates_ref, lags_ref, conv_ref):
        b_gate = dot(rows_ref[...], weight_ref[:chans, :], 1, 1)
        c_gate = dot(rows_ref[8:, :], weight_ref[chans : 2 * chans, :], 1, 1)
        x_gate = dot(rows_ref[...], weight_ref[2 * chans :, :], 1, 1)
        product = (b_gate * x_gate).astype(bf16).astype(f32)
        one = one_ref[...] * product[7 : 7 + own]
        two = two_ref[...] * product[6 : 6 + own]
        product = product[8:]
        gates_ref[0] = b_gate[8:]
        gates_ref[1] = c_gate
        gates_ref[2] = x_gate[8:]
        lags_ref[0] = product
        lags_ref[1] = one
        lags_ref[2] = two
        conv_ref[...] = taps_ref[0:1, :] * product + taps_ref[1:2, :] * one + taps_ref[2:3, :] * two

    operands = (rows, weight, taps, mask_one, mask_two)
    outs = [
        jax.ShapeDtypeStruct((3, own, chans), f32),
        jax.ShapeDtypeStruct((3, own, chans), f32),
        jax.ShapeDtypeStruct((own, chans), f32),
    ]
    return pl.pallas_call(
        body,
        grid=(1,),
        in_specs=whole(*(x.shape for x in operands)),
        out_specs=whole(*(x.shape for x in outs)),
        out_shape=outs,
        compiler_params=pltpu.CompilerParams(vmem_limit_bytes=28 * 1024 * 1024),
        cost_estimate=pl.CostEstimate(
            flops=6 * own * width * chans, bytes_accessed=6 * width * chans, transcendentals=0
        ),
        name="mixer_gates",
    )(*operands)


def residual_back(own_sums, moved, residual, inverse, gain, grad, weight, c_rows, mask_one, mask_two):
    own, width = residual.shape
    half = own // 2
    chans = weight.shape[0]

    def body(*refs):
        sums, moved_refs, refs = refs[:2], refs[2:8], refs[8:]
        res_ref, inv_ref, gain_ref, grad_ref, weight_ref, gates_ref, one_ref, two_ref = refs[:8]
        block_ref, d_res_ref, low_ref, part_ref, mixer_ref, edge_ref = refs[8:]
        parts = []
        for i in range(2):
            rows = slice(i * half, (i + 1) * half)
            total = sums[i][...]
            for part in moved_refs[3 * i : 3 * i + 3]:
                total = total + part[...].astype(f32)
            d_norm, ffn = total[:, :width], total[:, width:]
            res, inv = res_ref[rows, :], inv_ref[rows, :]
            block_ref[rows, :] = (res + ffn).astype(bf16)
            parts.append(jnp.sum(d_norm * res * inv, axis=0, keepdims=True))
            scaled = gain_ref[...] * d_norm
            mean = jnp.mean(scaled * res, axis=-1, keepdims=True)
            d_res = grad_ref[rows, :] + inv * (scaled - res * inv * inv * mean)
            d_res_ref[rows, :] = d_res
            low_ref[rows, :] = d_res.astype(bf16)
        part_ref[...] = parts[0] + parts[1]
        d_mixer = dot(low_ref[...], weight_ref[...], 1, 1)
        mixer_ref[...] = d_mixer
        d_conv = d_mixer[:8] * gates_ref[...]
        edge_ref[0:8, :] = one_ref[:8, :] * d_conv
        edge_ref[8:16, :] = two_ref[:8, :] * d_conv

    operands = (*own_sums, *moved, residual, inverse, gain, grad, weight, c_rows, mask_one, mask_two)
    outs = [
        jax.ShapeDtypeStruct((own, width), bf16),
        jax.ShapeDtypeStruct((own, width), f32),
        jax.ShapeDtypeStruct((own, width), bf16),
        jax.ShapeDtypeStruct((1, width), f32),
        jax.ShapeDtypeStruct((own, chans), f32),
        jax.ShapeDtypeStruct((16, chans), f32),
    ]
    return hbm_call(body, operands, outs, 60, 2 * own * width * chans, "residual_back")


def mixer_back(
    d_mixer, edges, gates, lags, conv, mask_one, mask_two, taps, weight, rows, gain, d_res, second, halves
):
    own, width = rows.shape
    chans = d_mixer.shape[1]
    per = chans // TPS
    extra = 2 * width // own + 8

    def body(*refs):
        mixer_ref, edge_ref, gates_ref, lags_ref, conv_ref, one_ref, two_ref = refs[:7]
        taps_ref, weight_ref, rows_ref, gain_ref, d_res_ref, second_ref, halves_ref = refs[7:14]
        out_ref, send_ref, grads_ref = refs[14:]
        d_mix = mixer_ref[...]
        d_conv = d_mix * gates_ref[1]
        lag_one = one_ref[...] * d_conv
        lag_two = two_ref[...] * d_conv
        ahead_one = jnp.concatenate([lag_one[1:], edge_ref[0:1, :]], axis=0)
        ahead_two = jnp.concatenate([lag_two[2:], edge_ref[8:10, :]], axis=0)
        d_product = (
            taps_ref[0:1, :] * d_conv + taps_ref[1:2, :] * ahead_one + taps_ref[2:3, :] * ahead_two
        )
        grads_ref[0] = (d_product * gates_ref[2]).astype(bf16)
        grads_ref[1] = (d_mix * conv_ref[...]).astype(bf16)
        grads_ref[2] = (d_product * gates_ref[0]).astype(bf16)
        d_norm = dot(grads_ref[0], weight_ref[:chans, :], 1, 0)
        d_norm = d_norm + dot(grads_ref[1], weight_ref[chans : 2 * chans, :], 1, 0)
        d_norm = d_norm + dot(grads_ref[2], weight_ref[2 * chans :, :], 1, 0)
        block = rows_ref[...]
        inverse = lax.rsqrt(jnp.mean(block * block, axis=-1, keepdims=True) + epsilon)
        first = jnp.sum(d_norm * block * inverse, axis=0, keepdims=True)
        scaled = gain_ref[...] * d_norm
        mean = jnp.mean(scaled * block, axis=-1, keepdims=True)
        out = d_res_ref[...] + inverse * (scaled - block * inverse * inverse * mean)
        out_ref[...] = out.astype(bf16)
        tap_sums = [jnp.sum(d_conv * lags_ref[k], axis=0, keepdims=True) for k in range(3)]
        sums = jnp.concatenate(tap_sums + [jnp.zeros((5, chans), f32)], axis=0)
        gains = []
        for value in (first, second_ref[...]):
            gains += [value[:, k * own : (k + 1) * own] for k in range(width // own)]
        gains = jnp.concatenate(gains, axis=0)
        for g in range(3):
            turned = grads_ref[g].astype(f32).T.astype(bf16)
            for j in range(TPS):
                send_ref[j, g * per : (g + 1) * per, :] = turned[j * per : (j + 1) * per]
        for j in range(TPS):
            pair = j // 2 * 2 * per
            tail = jnp.concatenate([gains, sums[:, pair : pair + 2 * per]], axis=0)
            send_ref[j, 3 * per : 3 * per + extra, :] = tail.astype(bf16)
            for k in range(width // own):
                at = 3 * per + extra + k * halves.shape[1]
                send_ref[j, at : at + halves.shape[1], :] = halves_ref[j, :, k * own : (k + 1) * own]

    operands = (d_mixer, edges, gates, lags, conv, mask_one, mask_two, taps, weight, rows, gain, d_res, second, halves)
    outs = [
        jax.ShapeDtypeStruct((own, width), bf16),
        jax.ShapeDtypeStruct((TPS, 3 * per + extra + halves.shape[1] * width // own, own), bf16),
    ]
    return pl.pallas_call(
        body,
        grid=(1,),
        in_specs=whole(*(x.shape for x in operands)),
        out_specs=whole(*(x.shape for x in outs)),
        out_shape=outs,
        scratch_shapes=[pltpu.VMEM((3, own, chans), bf16)],
        compiler_params=pltpu.CompilerParams(vmem_limit_bytes=36 * 1024 * 1024),
        cost_estimate=pl.CostEstimate(
            flops=6 * own * width * chans, bytes_accessed=6 * width * chans, transcendentals=0
        ),
        name="mixer_back",
    )(*operands)


def feed_forward(norms, d_hidden, start, gate_t, up_t, down, pieces):
    ff = d_hidden.shape[1]
    count = norms[0].shape[0] * len(norms)
    width = down.shape[1]
    step = norms[0].shape[0]
    piece = count // pieces

    def body(*refs):
        norm_refs, rest = refs[: len(norms)], refs[len(norms) :]
        d_hbm, gate_ref, up_ref, down_ref = rest[:4]
        outs, (d_gate_ref, d_up_ref, hidden_ref, d_ref, sem) = rest[4:-5], rest[-5:]
        load = pltpu.make_async_copy(d_hbm.at[pl.ds(start, count)], d_ref, sem)
        load.start()
        for k, norm_ref in enumerate(norm_refs):
            part = slice(k * step, (k + 1) * step)
            norm = norm_ref[...]
            gate = dot(norm, gate_ref[...], 1, 1)
            up = dot(norm, up_ref[...], 1, 1)
            if k == 0:
                load.wait()
            d_part = d_ref[part, :]
            sig = jax.nn.sigmoid(gate)
            act = gate * sig
            hidden = (act * up).astype(bf16)
            d_gate = (d_part * up * sig * (1.0 + gate * (1.0 - sig))).astype(bf16)
            d_up = (d_part * act).astype(bf16)
            d_gate_ref[part, :] = d_gate
            d_up_ref[part, :] = d_up
            hidden_ref[part, :] = hidden
            d_norm = (dot(d_gate, gate_ref[...], 1, 0) + dot(d_up, up_ref[...], 1, 0)).astype(bf16)
            ffn = dot(hidden, down_ref[...], 1, 0, bf16)
            first = k * step // piece
            for j in range(max(1, step // piece)):
                inside = slice(j * piece, (j + 1) * piece)
                outs[first + j][:, :width] = d_norm[inside]
                outs[first + j][:, width:] = ffn[inside]

    outs = pl.pallas_call(
        body,
        in_specs=in_vmem(len(norms)) + [pl.BlockSpec(memory_space=pltpu.HBM)] + in_vmem(3),
        out_specs=in_vmem(pieces + 3),
        out_shape=[jax.ShapeDtypeStruct((piece, 2 * width), bf16)] * pieces
        + [jax.ShapeDtypeStruct((count, ff), bf16)] * 3,
        scratch_shapes=[pltpu.VMEM((count, ff), f32), pltpu.SemaphoreType.DMA(())],
        compiler_params=pltpu.CompilerParams(vmem_limit_bytes=12 * 1024 * 1024),
        cost_estimate=pl.CostEstimate(
            flops=10 * count * width * ff,
            bytes_accessed=count * width * 6,
            transcendentals=count * ff,
        ),
        name="feed_forward",
    )(*norms, d_hidden, gate_t, up_t, down)
    return outs[:pieces], outs[pieces:]


def dot(left, right, left_dim, right_dim, kind=f32):
    out = lax.dot_general(
        left, right, (((left_dim,), (right_dim,)), ((), ())), preferred_element_type=f32
    )
    return out.astype(kind)


def doc_index(doc_starts, positions):
    hits = (doc_starts[:, None, :] <= positions[None, :, None]).astype(jnp.int32)
    return jnp.sum(hits, axis=-1) - 1


def shards(
    block_input,
    first_gain,
    in_weight,
    conv_taps,
    out_weight,
    second_gain,
    gate_weight,
    up_weight,
    down_weight,
    doc_starts,
    out_cotangent,
):
    seqs, seg, width = block_input.shape
    chans = in_weight.shape[2]
    ff = gate_weight.shape[1]
    count = seqs * seg
    own = count // TPS
    per_seq = TPS // seqs
    y, x = lax.axis_index("y"), lax.axis_index("x")
    place = y * RING + x
    seq = lax.axis_index(SEQ)
    starts = plane_starts(own // 2)

    positions = seq * seg + jnp.arange(seg, dtype=jnp.int32)
    current = doc_index(doc_starts, positions)
    one_back = (doc_index(doc_starts, positions - 1) == current).astype(f32)
    two_back = (doc_index(doc_starts, positions - 2) == current).astype(f32)

    channels = TPS * chans
    is_low = lax.axis_index("core") == 0
    out_half = lax.dynamic_slice_in_dim(
        out_weight, lax.axis_index("core") * (chans // 2), chans // 2, axis=0
    )
    out_mine = jnp.broadcast_to(out_half[None], (TPS, chans // 2, width))
    out_mine = lax.all_to_all(out_mine, TP, 0, 0, tiled=True)
    in_wt = jnp.transpose(in_weight, (1, 2, 0))
    share = chans // 8
    taps_high = lax.reduce_precision(conv_taps, 8, 7)
    taps_mid = lax.reduce_precision(conv_taps - taps_high, 8, 7)
    taps_low = lax.reduce_precision(conv_taps - taps_high - taps_mid, 8, 7)
    taps_row = jnp.stack([taps_high, taps_mid, taps_low], axis=0).astype(bf16).reshape(1, 9 * chans)
    taps_row = jnp.pad(taps_row, ((0, share - 1), (0, width - 9 * chans)))
    in_share = lax.dynamic_slice_in_dim(in_wt, seq * share, share, axis=1)
    in_share = jnp.concatenate([in_share, taps_row[None]], axis=0)
    in_all = lax.all_gather(in_share, ALL, axis=0, tiled=False)
    in_all = in_all.reshape(8, TPS, 4, share, width)
    taps = in_all[0, :, 3, 0, : 9 * chans].astype(f32).reshape(TPS, 3, 3, chans)
    taps = (taps[:, 0] + taps[:, 1]) + taps[:, 2]
    taps = taps.transpose(1, 0, 2).reshape(3, channels)
    in_all = in_all[:, :, :3].transpose(2, 1, 0, 3, 4).reshape(3 * channels, width)

    flat_input = block_input.reshape(count, width)
    in_flat = in_wt.reshape(3 * chans, width)
    normed1, projected = norm_and_project(flat_input, first_gain, in_flat)
    projected, out_mine = tied((projected, out_mine))
    out_theirs = swap_cores(out_mine)
    out_all = jnp.stack(
        [jnp.where(is_low, out_mine, out_theirs), jnp.where(is_low, out_theirs, out_mine)], axis=1
    ).reshape(channels, width)
    last = normed1.reshape(seqs, seg, width)[:, seg - 8 :]
    carried = lax.ppermute(
        last, ALL, [(i, i + TPS) for i in range(7 * TPS)]
    )
    mixer_blocks = []
    for s in range(seqs):
        proj = projected[:, s * seg : (s + 1) * seg]
        edge = dot(in_flat, carried[s], 1, 1)
        product = (proj[:chans] * proj[2 * chans :]).astype(bf16)
        before = (edge[:chans] * edge[2 * chans :]).astype(bf16)
        extended = jnp.concatenate([before[:, 6:], product], axis=1).astype(f32)
        convolved = (
            conv_taps[0][:, None] * product.astype(f32)
            + conv_taps[1][:, None] * one_back[s] * extended[:, 1 : seg + 1]
            + conv_taps[2][:, None] * two_back[s] * extended[:, :seg]
        )
        mixed = (proj[chans : 2 * chans] * convolved).astype(bf16)
        mixer_blocks.append(mixed.reshape(chans, per_seq, own).transpose(1, 0, 2))
    mixer_blocks = jnp.concatenate(mixer_blocks, axis=0)
    mixer = lax.all_to_all(mixer_blocks, TP, 0, 0, tiled=True)
    mixer = mixer.reshape(channels, own)

    rows_in = lax.dynamic_slice_in_dim(flat_input, place * own, own, axis=0)
    residual = rows_in + dot(mixer, out_all, 0, 0)
    inverse_two = lax.rsqrt(jnp.mean(residual * residual, axis=-1, keepdims=True) + epsilon)
    normed2 = (residual * inverse_two * second_gain).astype(bf16)

    later = (normed2[0, 0].astype(f32) * 0.0).astype(jnp.int32)
    split = count * 3 // 4
    *grad_low, hidden_first, hidden_last = relative_rows(
        out_cotangent.reshape(count, width), starts + later, down_weight, split
    )
    gate_t, up_t = gate_weight.T, up_weight.T
    quarter = count // 4
    norm_first, norm_last, _, _, ((near_hidden, hidden_last), own_results) = plane_gather(
        normed2,
        beside=(hidden_first, hidden_last),
        own=lambda norms: feed_forward(norms, hidden_first, 0, gate_t, up_t, down_weight, 2),
    )
    sums_own, kept_own = own_results
    sums_near, kept_near = feed_forward(
        norm_first[2:], near_hidden, quarter, gate_t, up_t, down_weight, 4
    )
    piece = norm_last[0].shape[0]
    norm_last = assemble(
        norm_last, (((0, 0, piece), (1, 0, piece)), ((2, 0, piece), (3, 0, piece)))
    )
    norm_last, sums_near = tied((norm_last, sums_near))
    sums_last, kept_last = feed_forward(norm_last, hidden_last, 0, gate_t, up_t, down_weight, 4)
    moved = scatter_far(sums_last, ("y", "x"))
    moved, kept_own, kept_near, kept_last, norm_first, norm_last = tied(
        (moved, kept_own, kept_near, kept_last, norm_first, norm_last)
    )
    rows = norm_last[0].shape[0]
    norm_parts = assemble(
        tuple(norm_first) + tuple(norm_last),
        tuple(tuple((i, 0, rows) for i in group) for group in ((0, 1), (2, 3, 4, 5), (6, 7))),
    )
    low_parts = (grad_low[0][:quarter], grad_low[0][quarter:], grad_low[1])
    ffn_grads = []
    for k in range(3):
        rights = norm_parts if k < 2 else low_parts
        part = sum(
            dot(kept[k], right, 0, 0)
            for kept, right in zip((kept_own, kept_near, kept_last), rights)
        )
        ffn_grads.append(part.astype(bf16))
    ffn_grads = jnp.concatenate(ffn_grads + [jnp.zeros((32, width), bf16)], axis=0)
    ffn_grads = lax.psum_scatter(ffn_grads, SEQ, scatter_dimension=0, tiled=True)

    rows_n1 = lax.dynamic_slice_in_dim(normed1, place * own, own, axis=0)
    local_edge = lax.dynamic_slice_in_dim(normed1, place * own - 8, 8, axis=0)
    at_start = place % per_seq == 0
    edge_n1 = jnp.where(at_start, carried[place // per_seq], local_edge)
    rows_one = lax.dynamic_slice_in_dim(one_back.reshape(count, 1), place * own, own, axis=0)
    rows_two = lax.dynamic_slice_in_dim(two_back.reshape(count, 1), place * own, own, axis=0)
    rows_n1 = jnp.concatenate([edge_n1, rows_n1], axis=0)

    moved = scatter_near(list(sums_near), moved, ("y", "x"))
    gates, lags, conv = mixer_gates(rows_n1, in_all, taps, rows_one, rows_two)
    moved, gates, lags, conv = tied((moved, gates, lags, conv))
    top = ring_sums(sums_own[0], *moved[:2])
    bottom = ring_sums(sums_own[1], *moved[2:])
    moved = tuple(turn(top[k], "x", k) for k in (1, 2, 3))
    moved = moved + tuple(turn(bottom[k], "y", k) for k in (1, 2, 3))
    moved, ffn_grads = tied((moved, ffn_grads))

    grad_rows = lax.dynamic_slice_in_dim(
        out_cotangent.reshape(count, width), place * own, own, axis=0
    )
    block_rows, d_residual, d_low, second_part, d_mixer, edges = residual_back(
        (top[0], bottom[0]),
        moved,
        residual,
        inverse_two,
        second_gain.reshape(1, width),
        grad_rows,
        out_all,
        gates[1, :8],
        rows_one,
        rows_two,
    )
    block_output = lax.all_gather(block_rows, TP, axis=0, tiled=True)
    pairs = []
    for sq in range(8):
        for j in range(TPS):
            if j % per_seq:
                pairs.append((sq * TPS + j, sq * TPS + j - 1))
            elif sq:
                pairs.append((sq * TPS + j, (sq - 1) * TPS + j + per_seq - 1))
    edges = lax.ppermute(edges, ALL, pairs)
    out_part = dot(mixer, d_low, 1, 0, bf16).reshape(TPS, 2, chans // 2, width)
    theirs = swap_cores(jnp.where(is_low, out_part[:, 1], out_part[:, 0]))
    out_part = jnp.where(is_low, out_part[:, 0], out_part[:, 1]).astype(f32) + theirs.astype(f32)
    input_rows, exchanged = mixer_back(
        d_mixer,
        edges,
        gates,
        lags,
        conv,
        rows_one,
        rows_two,
        taps,
        in_all,
        rows_in,
        first_gain.reshape(1, width),
        d_residual,
        second_part,
        out_part.astype(bf16),
    )
    middle = 3 * chans // 2

    def exchange(early):
        exchanged, ffn_grads = early
        exchanged = lax.all_to_all(exchanged, TP, 0, 0, tiled=True)
        return exchanged, lax.all_gather(ffn_grads, SEQ, axis=0, tiled=True)

    input_first, input_last, exchanged, ffn_grads, block_output = plane_gather(
        input_rows, (exchanged, ffn_grads), exchange, block_output
    )
    received = exchanged[:, : 3 * chans].transpose(1, 0, 2)
    in_part = dot(received.reshape(3 * chans, count), normed1, 1, 0, bf16)
    small = jnp.sum(exchanged[:, 3 * chans :].astype(f32), axis=0).astype(bf16)
    out_part = small[24:].reshape(width // own, chans // 2, own).transpose(1, 0, 2)
    out_part = out_part.reshape(chans // 2, width)
    small = jnp.pad(small[:24].reshape(3, width), ((0, 5), (0, 0)))
    theirs = swap_cores(
        jnp.concatenate([jnp.where(is_low, in_part[middle:], in_part[:middle]), small], axis=0)
    )
    mine = jnp.where(is_low, in_part[:middle], in_part[middle:])
    mine = jnp.concatenate([mine, small], axis=0).astype(f32) + theirs.astype(f32)
    mine = jnp.concatenate([mine.astype(bf16), out_part], axis=0)
    by_z = jnp.broadcast_to(mine[None], (RING,) + mine.shape)
    by_z = lax.all_to_all(by_z, "z", 0, 0, tiled=True)
    block_output = block_output.astype(f32)
    gate_grad = ffn_grads[:ff].astype(f32).T
    up_grad = ffn_grads[ff : 2 * ff].astype(f32).T
    down_grad = ffn_grads[2 * ff : 3 * ff].astype(f32)
    input_grad = absolute_rows(input_first + input_last, starts)

    by_z = by_z.astype(f32)
    total = (by_z[0] + by_z[2]) + (by_z[1] + by_z[3])
    small = total[middle : middle + 8]
    mine = jnp.concatenate([total[:middle], total[middle + 8 :]], axis=0).astype(bf16)
    theirs = swap_cores(mine)
    low, high = jnp.where(is_low, mine, theirs), jnp.where(is_low, theirs, mine)
    low, high = low.astype(f32), high.astype(f32)
    in_grad = jnp.concatenate([low[:middle], high[:middle]], axis=0)
    in_grad = in_grad.reshape(3, chans, width).transpose(2, 0, 1)
    out_grad = jnp.concatenate([low[middle:], high[middle:]], axis=0)
    first_grad, second_grad = small[0], small[1]
    taps_grad = small[2].reshape(8, own)[:3]
    taps_grad = lax.dynamic_slice_in_dim(taps_grad, place % 2 * chans, chans, axis=1)

    return (
        block_output.reshape(seqs, seg, width),
        input_grad.reshape(seqs, seg, width),
        first_grad,
        in_grad,
        taps_grad,
        out_grad,
        second_grad,
        gate_grad,
        up_grad,
        down_grad,
    )


def solution(mesh):
    grid = Mesh(mesh.devices.reshape(4, 2, RING, RING), ALL)
    return jax.shard_map(
        shards,
        mesh=grid,
        in_specs=(
            P(None, SEQ, None),
            P(),
            P(None, None, TP),
            P(None, TP),
            P(TP, None),
            P(),
            P(None, TP),
            P(None, TP),
            P(TP, None),
            P(),
            P(None, SEQ, None),
        ),
        out_specs=(
            P(None, SEQ, None),
            P(None, SEQ, None),
            P(),
            P(None, None, TP),
            P(None, TP),
            P(TP, None),
            P(),
            P(None, TP),
            P(None, TP),
            P(TP, None),
        ),
        check_vma=False,
    )
```
